32 devices in a mesh: groups: 2 (over y), cubes: 16 (over z, x, core).
Axes of the slice: x: 2, y: 2, z: 4, core: 2. Of those that a mesh axis runs over, the one named last changes fastest.
Arguments:
- query_rows: bfloat16 [4096, 2560], P(('groups', 'cubes')), parts along dimension 0, may hold values from -8 to 8
- key_rows: bfloat16 [4096, 2560], P(('groups', 'cubes')), parts along dimension 0, may hold values from -9 to 9
- value_rows: bfloat16 [4096, 2560], P(('groups', 'cubes')), parts along dimension 0, may hold values from -6 to 6
- gate_logits: bfloat16 [4096, 40], P(('groups', 'cubes')), parts along dimension 0, may hold values from -6 to 6
- selection: int32 [64, 20, 8], P('groups'), parts along dimension 0, may hold values from 0 to 31, all different within a row; in each aligned block of 40 rows (0 to 39, 40 to 79, ..., all dimensions but the last counted through in order) at most 11 rows name the same one
- cube_ids: int32 [64], P('groups'), parts along dimension 0, may hold values from 0 to 31, each once
Outputs:
- mixed: bfloat16 [4096, 2560], P(('groups', 'cubes')), parts along dimension 0
The draws below stay inside these ranges and needn't reach their ends.
There are 2 independent parts, one for each index of `groups`. The reference program is written for one: setup_inputs(seed, part) draws one part's arguments, and reference() takes and returns one part's arrays. A program takes and returns all parts, laid end to end along the dimension named above; each array names one. Nothing has to cross between parts.
Inputs may be any that keep to these rules, and one draw needn't show every extreme that they name: `selection`: each row of 8 names different cubes. Among the rows of one device (its 2 stored blocks with all 20 heads) no cube is named more than 11 times, a bound that some block reaches. `cube_ids`: each cube number appears once.
All inputs are finite; a program needn't handle non-finite values.
Results may differ from the reference program's by a relative error of at most 0.0047.
Values may be sent and summed in bfloat16 or wider, within the bound.
A program may use at most 128 MiB of HBM per device.

```python
import math
import jax
import jax.numpy as jnp
import numpy as np
from jax import lax

HEADS = 20
HDIM = 128
CUBE = 64
TOPK = 8
CUBE_DEV = 2
NC = 32
TOKENS = 2048
MOST = 11


def shared_part(key, salt):
    cube_key, token_key = jax.random.split(jax.random.fold_in(key, salt))
    shared = jnp.clip(jax.random.normal(cube_key, (NC, 1, HEADS * HDIM), jnp.float32), -4.0, 4.0) * 0.8
    return (shared, token_key)


def cube_rows(key, salt):
    shared, token_key = shared_part(key, salt)
    single = jnp.clip(jax.random.normal(token_key, (NC, CUBE, HEADS * HDIM), jnp.float32), -4.0, 4.0) * 0.6
    return shared + single


def draw_key_rows(key, part):
    values = cube_rows(key, 11)
    return values.reshape(TOKENS, HEADS * HDIM).astype(jnp.bfloat16)


def draw_value_rows(key, part):
    values = cube_rows(key, 17)
    return values.reshape(TOKENS, HEADS * HDIM).astype(jnp.bfloat16)


def draw_query_rows(key, part):
    normal_key = jax.random.fold_in(jax.random.fold_in(key, 13), 0)
    noise = jnp.clip(jax.random.normal(normal_key, (NC, CUBE, HEADS * HDIM), jnp.float32), -4.0, 4.0) * 0.7
    key_shared, unused = shared_part(key, 11)
    earlier = jnp.roll(key_shared, CUBE_DEV, axis=0)
    values = (noise + 1.5 * earlier).reshape(TOKENS, HEADS * HDIM)
    return values.astype(jnp.bfloat16)


def block_levels(key, dims, pieces, low, high):
    def one(dim, blocks):
        heights = jax.random.uniform(jax.random.fold_in(jax.random.fold_in(key, 6), dim), (blocks,), jnp.float32, low / len(pieces), high / len(pieces))
        return jnp.repeat(jnp.exp(heights), dims[dim] // blocks).reshape((-1,) + (1,) * (len(dims) - dim - 1))

    level = one(*pieces[0])
    for cut in pieces[1:]:
        level = level * one(*cut)
    return level


def deal_out(stream_key, own, number, rows, amount, top, most, slope):
    order = jax.random.permutation(stream_key, amount)
    crowded, common = load_shares(amount, rows * top, most, slope, True), load_shares(amount, rows * top, most, slope, False)
    places = jnp.arange(amount)

    def named(lengths, turn):
        used = int((lengths > 0).sum())
        fixed = max(1, used // 4)
        shifted = fixed + (places - fixed + turn * (used - fixed)) % max(1, amount - fixed)
        return jnp.zeros((amount,), jnp.int32).at[order[jnp.where(places < fixed, places, shifted)]].set(jnp.asarray(lengths, jnp.int32))

    lengths = jnp.where(number % 4 == 0, named(crowded, number // 4), named(common, number - number // 4 - 1))
    mixed = jax.random.permutation(jax.random.fold_in(own, 3), amount)
    source_of, sink = mixed[0:amount // 2 * 2:2], mixed[1:amount // 2 * 2:2]
    slack = jnp.minimum(lengths[source_of] - 1, most - lengths[sink]) // 2
    slack = jnp.where((source_of == order[0]) | (sink == order[0]) | (lengths[sink] == 0), 0, jnp.maximum(slack, 0))
    shifted = jax.random.randint(jax.random.fold_in(own, 4), (amount // 2,), 0, 1 << 20) % (slack + 1)
    lengths = lengths.at[source_of].add(-shifted).at[sink].add(shifted)
    items = jnp.searchsorted(jnp.cumsum(lengths), jnp.arange(rows * top), side="right").astype(jnp.int32)
    table = items.reshape(top, rows).T
    table = table[jax.random.permutation(jax.random.fold_in(own, 1), rows)]
    turn = jax.random.randint(jax.random.fold_in(own, 2), (rows, 1), 0, top)
    return jnp.take_along_axis(table, (jnp.arange(top)[None, :] + turn) % top, axis=1)


def load_shares(amount, total, reach, skew, full):
    loads = [(1 << 20) // math.isqrt(rank ** skew) + 1 for rank in range(1, amount + 1)]
    largest = reach if full else min(reach, max(-(-total // amount), total * loads[0] // sum(loads)))
    least = 1 if total - largest >= amount - 1 else 0
    holding, rest = [largest] + [least] * (amount - 1), total - largest - least * (amount - 1)
    while rest > 0:
        free = [i for i in range(1, amount) if holding[i] < largest] or [i for i in range(1, amount) if holding[i] < reach]
        whole, budget = sum([loads[i] for i in free]), rest
        for i in free:
            extra = min(reach - holding[i], max(1, budget * loads[i] // whole), rest)
            holding[i] = holding[i] + extra
            rest = rest - extra
    return np.array(holding)


def gaussian(key, dims, deviation, bound, pieces=(), held_as=jnp.bfloat16):
    entries = deviation * jax.random.normal(key, dims, jnp.float32)
    if pieces:
        entries = entries * block_levels(key, dims, pieces, -0.22, 0.18)
    return jnp.clip(entries, -bound, bound).astype(held_as)


def setup_inputs(seed: int = 0, part: int = 0) -> dict:
    streams_of = jax.random.split(jax.random.key(seed), 7)
    own_keys = jax.random.split(jax.random.fold_in(streams_of[6], part), 7)
    query_rows = draw_query_rows(jax.random.fold_in(jax.random.fold_in(streams_of[6], part), 71), part)
    key_rows = draw_key_rows(jax.random.fold_in(jax.random.fold_in(streams_of[6], part), 71), part)
    value_rows = draw_value_rows(jax.random.fold_in(jax.random.fold_in(streams_of[6], part), 71), part)
    gate_logits = gaussian(own_keys[3], (TOKENS, 2 * HEADS), 1.5, 6.0, ((0, 16),))
    selection_keys = jax.random.split(jax.random.fold_in(own_keys[4], 1), NC * HEADS // (CUBE_DEV * HEADS))
    selection_turns = jax.random.permutation(jax.random.fold_in(own_keys[4], 3), NC * HEADS // (CUBE_DEV * HEADS))
    selection = jax.vmap(lambda own, number: deal_out(jax.random.fold_in(own_keys[4], 2), own, number, CUBE_DEV * HEADS, NC, TOPK, MOST, 2))(selection_keys, selection_turns).reshape((NC, HEADS, TOPK))
    cube_ids = jax.random.permutation(own_keys[5], NC).astype(jnp.int32)
    return {"query_rows": query_rows, "key_rows": key_rows, "value_rows": value_rows, "gate_logits": gate_logits, "selection": selection, "cube_ids": cube_ids}


def reference(query_rows, key_rows, value_rows, gate_logits, selection, cube_ids):
    factor = 1.0 / math.sqrt(HDIM)
    feature_width = HEADS * HDIM
    pooled_key = lax.optimization_barrier(jnp.mean(key_rows.astype(jnp.float32).reshape(NC, CUBE, feature_width), axis=1)).astype(jnp.bfloat16)
    pooled_value = lax.optimization_barrier(jnp.mean(value_rows.astype(jnp.float32).reshape(NC, CUBE, feature_width), axis=1)).astype(jnp.bfloat16)
    pooled_keys = lax.optimization_barrier(pooled_key).astype(jnp.float32).reshape(NC, HEADS, HDIM)
    pooled_values = lax.optimization_barrier(pooled_value).astype(jnp.float32).reshape(NC, HEADS, HDIM)
    query_blocks = query_rows.reshape(NC, CUBE, HEADS, HDIM)
    key_blocks = key_rows.reshape(NC, CUBE, HEADS, HDIM).transpose(0, 2, 1, 3)
    value_blocks = value_rows.reshape(NC, CUBE, HEADS, HDIM).transpose(0, 2, 1, 3)
    cube_range = jnp.arange(NC, dtype=jnp.int32)
    position = lax.optimization_barrier(jnp.sum(jnp.where(cube_ids[None, :] == cube_range[:, None], cube_range[None, :], 0), axis=1)).astype(jnp.int32)
    targets = jnp.take(position, selection.reshape(-1)).reshape(NC, HEADS, TOPK).astype(jnp.int32)
    head_range = jnp.arange(HEADS, dtype=jnp.int32)

    def one_block(inputs):
        queries, chosen = inputs
        query_float = queries.astype(jnp.float32)
        coarse_scores = jnp.einsum('thd,jhd->htj', query_float, pooled_keys) * factor
        coarse_weights = jnp.exp(coarse_scores - lax.optimization_barrier(jnp.max(coarse_scores, axis=2, keepdims=True)))
        coarse_rounded = lax.optimization_barrier(coarse_weights.astype(jnp.bfloat16)).astype(jnp.float32)
        coarse = jnp.einsum('htj,jhd->thd', coarse_rounded, pooled_values)
        coarse = coarse / lax.optimization_barrier(jnp.sum(coarse_weights, axis=2)).T[:, :, None]
        fine_keys = key_blocks[chosen, head_range[:, None]].reshape(HEADS, TOPK * CUBE, HDIM).astype(jnp.float32)
        fine_values = value_blocks[chosen, head_range[:, None]].reshape(HEADS, TOPK * CUBE, HDIM).astype(jnp.float32)
        fine_scores = jnp.einsum('thd,hkd->htk', query_float, fine_keys) * factor
        fine_weights = jnp.exp(fine_scores - lax.optimization_barrier(jnp.max(fine_scores, axis=2, keepdims=True)))
        fine_rounded = lax.optimization_barrier(fine_weights.astype(jnp.bfloat16)).astype(jnp.float32)
        fine = jnp.einsum('htk,hkd->thd', fine_rounded, fine_values)
        fine = fine / lax.optimization_barrier(jnp.sum(fine_weights, axis=2)).T[:, :, None]
        return (coarse, fine)
    coarse, fine = lax.map(one_block, (query_blocks, targets))
    gates = jax.nn.sigmoid(gate_logits.astype(jnp.float32)).reshape(NC, CUBE, 2, HEADS)
    mixed = gates[:, :, 0, :, None] * coarse + gates[:, :, 1, :, None] * fine
    return mixed.reshape(NC * CUBE, feature_width).astype(jnp.bfloat16)
```

```python
import functools
import math

import jax
import jax.numpy as jnp
from jax import lax
from jax.experimental import pallas as pl
from jax.experimental.pallas import tpu as pltpu
from jax.sharding import PartitionSpec as P

CUBE = 64
HEADS_PER_CHUNK = 4
LOOKAHEAD = 2


def X_FIRST(chunk_count):
    return (chunk_count // 2,)


NEG_START = -1e30


def block_partials(query_slots, pair_slots):
    head_size = query_slots.shape[-1]
    factor = 1.0 / math.sqrt(head_size)
    slot_keys = pair_slots[:, :, :head_size]
    slot_values = pair_slots[:, :, head_size:]
    scores = (
        jnp.einsum("sqd,skd->sqk", query_slots, slot_keys, preferred_element_type=jnp.float32)
        * factor
    )
    slot_max = jnp.max(scores, axis=2)
    weights = jnp.exp(scores - slot_max[:, :, None])
    slot_total = jnp.sum(weights, axis=2)
    numerator = jnp.einsum(
        "sqk,skd->sqd",
        weights.astype(jnp.bfloat16),
        slot_values,
        preferred_element_type=jnp.float32,
    )
    return (numerator, slot_max, slot_total)


def merge_slots(state, results, slot_group):
    numerator, running_max, totals = state
    slot_numerator, slot_max, slot_total = results
    group_count = numerator.shape[0]
    slot_count = slot_group.shape[0]
    member = slot_group[:, None] == jnp.arange(group_count, dtype=jnp.int32)[None, :]
    is_valid = slot_group >= 0
    group_max = jnp.max(jnp.where(member[:, :, None], slot_max[:, None, :], -jnp.inf), axis=0)
    new_max = jnp.maximum(running_max, group_max)
    slot_base = jnp.take(new_max, jnp.maximum(slot_group, 0), axis=0)
    slot_weight = jnp.exp(jnp.where(is_valid[:, None], slot_max - slot_base, -jnp.inf))
    onehot = member.astype(jnp.float32).T
    weighted = (slot_weight[:, :, None] * slot_numerator).reshape(slot_count, -1)
    added_numerator = jnp.dot(onehot, weighted, precision=lax.Precision.HIGHEST).reshape(
        numerator.shape
    )
    added_total = jnp.dot(onehot, slot_weight * slot_total, precision=lax.Precision.HIGHEST)
    decay_factor = jnp.exp(running_max - new_max)
    return (
        numerator * decay_factor[:, :, None] + added_numerator,
        new_max,
        totals * decay_factor + added_total,
    )


def streamed_body(query_rows, key_rows, value_rows, gate_logits, selection, cube_ids):
    device_count = lax.axis_size("cubes")
    token_count = query_rows.shape[0]
    feature_width = query_rows.shape[1]
    head_count = gate_logits.shape[1] // 2
    head_size = feature_width // head_count
    local_cubes = token_count // CUBE
    total_cubes = cube_ids.shape[0]
    picks_each = selection.shape[2]
    depth_rounds = max(2, head_count * picks_each // device_count + 1)
    request_count = local_cubes * head_count * picks_each
    factor = 1.0 / math.sqrt(head_size)
    self_index = lax.axis_index("cubes")
    pooled_keys = jnp.mean(
        key_rows.reshape(local_cubes, CUBE, feature_width), axis=1, dtype=jnp.float32
    ).astype(jnp.bfloat16)
    pooled_values = jnp.mean(
        value_rows.reshape(local_cubes, CUBE, feature_width), axis=1, dtype=jnp.float32
    ).astype(jnp.bfloat16)
    query_heads = query_rows.reshape(token_count, head_count, head_size)
    start_state = (
        jnp.zeros((head_count, token_count, head_size), jnp.float32),
        jnp.full((head_count, token_count), NEG_START, jnp.float32),
        jnp.zeros((head_count, token_count), jnp.float32),
    )
    numerator, running_max, totals = start_state
    piece_keys = lax.all_gather(pooled_keys, "cubes", axis=0, tiled=True)
    piece_values = lax.all_gather(pooled_values, "cubes", axis=0, tiled=True)
    piece_rows = piece_keys.shape[0]
    scores = (
        jnp.einsum(
            "thd,jhd->htj",
            query_heads,
            piece_keys.reshape(piece_rows, head_count, head_size),
            preferred_element_type=jnp.float32,
        )
        * factor
    )
    new_max = jnp.maximum(running_max, jnp.max(scores, axis=2))
    weights = jnp.exp(scores - new_max[:, :, None])
    added = jnp.einsum(
        "htj,jhd->htd",
        weights.astype(jnp.bfloat16),
        piece_values.reshape(piece_rows, head_count, head_size),
        preferred_element_type=jnp.float32,
    )
    numerator = added
    totals = jnp.sum(weights, axis=2)
    coarse = jnp.transpose(numerator / totals[:, :, None], (1, 0, 2))
    cube_range = jnp.arange(total_cubes, dtype=jnp.int32)
    position = jnp.sum(
        jnp.where(cube_ids[None, :] == cube_range[:, None], cube_range[None, :], 0), axis=1
    )
    targets = jnp.take(position, selection.reshape(-1)).reshape(device_count, request_count)
    request_range = jnp.arange(request_count, dtype=jnp.int32)
    request_group = request_range // picks_each
    request_head = request_group % head_count
    round_range = jnp.arange(depth_rounds, dtype=jnp.int32)
    own_targets = lax.dynamic_index_in_dim(targets, self_index, 0, keepdims=False)
    same_target = own_targets[:, None] == cube_range[None, :]
    running_count = jnp.cumsum(same_target.astype(jnp.int32), axis=0)
    own_rank = jnp.sum(jnp.where(same_target, running_count, 0), axis=1) - 1
    chosen_round = same_target[None, :, :] & (own_rank[None, :, None] == round_range[:, None, None])
    wanted_all = jnp.sum(jnp.where(chosen_round, request_group[None, :, None] + 1, 0), axis=1) - 1
    own_cubes = self_index * local_cubes + jnp.arange(local_cubes, dtype=jnp.int32)
    hit_mine = targets[:, :, None] == own_cubes[None, None, :]
    mine_rank = jnp.cumsum(hit_mine.astype(jnp.int32), axis=1) - 1
    round_hit = hit_mine[None] & (mine_rank[None] == round_range[:, None, None, None])
    incoming_all = (
        jnp.sum(jnp.where(round_hit, request_head[None, None, :, None] + 1, 0), axis=2) - 1
    )
    query_groups = (
        query_rows.reshape(local_cubes, CUBE, head_count, head_size)
        .transpose(0, 2, 1, 3)
        .reshape(local_cubes * head_count, CUBE, head_size)
    )
    pair_blocks = jnp.concatenate(
        (
            key_rows.reshape(local_cubes, CUBE, head_count, head_size),
            value_rows.reshape(local_cubes, CUBE, head_count, head_size),
        ),
        axis=3,
    )
    pair_groups = pair_blocks.transpose(0, 2, 1, 3).reshape(
        local_cubes * head_count, CUBE, 2 * head_size
    )
    base_group = head_count * jnp.arange(local_cubes, dtype=jnp.int32)

    def held_pairs(incoming):
        source = (jnp.maximum(incoming, 0) + base_group[None, :]).reshape(-1)
        picked = jnp.take(pair_groups, source, axis=0)
        return jnp.where(
            (incoming >= 0).reshape(-1)[:, None, None], picked, jnp.zeros((), jnp.bfloat16)
        )

    def asked_queries(wanted):
        picked = jnp.take(query_groups, jnp.maximum(wanted, 0), axis=0)
        return jnp.where((wanted >= 0)[:, None, None], picked, jnp.zeros((), jnp.bfloat16))

    def one_round(state, tables):
        wanted, incoming = tables
        arrived = lax.all_to_all(
            held_pairs(incoming), "cubes", split_axis=0, concat_axis=0, tiled=True
        )
        results = block_partials(asked_queries(wanted), arrived)
        return (merge_slots(state, results, wanted), None)

    group_count = local_cubes * head_count
    start_state = (
        jnp.zeros((group_count, CUBE, head_size), jnp.float32),
        jnp.full((group_count, CUBE), NEG_START, jnp.float32),
        jnp.zeros((group_count, CUBE), jnp.float32),
    )
    final_state, unused = lax.scan(one_round, start_state, (wanted_all, incoming_all))
    numerator, running_max, totals = final_state
    fine_groups = numerator / totals[:, :, None]
    fine = (
        fine_groups.reshape(local_cubes, head_count, CUBE, head_size)
        .transpose(0, 2, 1, 3)
        .reshape(token_count, head_count, head_size)
    )
    gates = jax.nn.sigmoid(gate_logits.astype(jnp.float32))
    mixed = gates[:, :head_count, None] * coarse + gates[:, head_count:, None] * fine
    return mixed.reshape(token_count, feature_width).astype(jnp.bfloat16)

CORES = 2
TILE_ROWS = 16
VMEM_BUDGET = 40 * 1024 * 1024


def grid_of(device_count):
    chips = device_count // CORES
    x_extent = 1
    for extent in range(1, chips + 1):
        if chips % extent == 0 and extent**3 <= chips:
            x_extent = extent
    return (chips // x_extent, x_extent)


def head_chunks(head_count):
    chunk_heads = HEADS_PER_CHUNK if head_count % HEADS_PER_CHUNK == 0 else 1
    chunk_count = head_count // chunk_heads
    return (chunk_heads, chunk_count, set(X_FIRST(chunk_count)))


def attention_kernel(
    sizes, target_ref, query_ref, key_ref, value_ref, gate_ref, out_ref, *scratch
):
    device_count, head_count, head_size, local_cubes, picks = sizes
    chunk_heads, chunk_count, x_first = head_chunks(head_count)
    z_extent, x_extent = grid_of(device_count)
    buffers = scratch[:chunk_count]
    pool_ref = scratch[chunk_count]
    send_sem, recv_sem = scratch[chunk_count + 1 :]
    width = chunk_heads * head_size
    token_count = query_ref.shape[0]
    factor = 1.0 / math.sqrt(head_size)
    z_stride = x_extent * CORES
    me = lax.axis_index("cubes")
    z = me // z_stride
    x = (me // CORES) % x_extent
    core = me % CORES
    sibling = me + 1 - 2 * core
    across = me + CORES * (1 - 2 * x)
    has_up = z < z_extent - 1
    has_down = z > 0
    partners = {
        "up": (me + z_stride, has_up),
        "down": (me - z_stride, has_down),
        "across": (across, None),
        "sibling": (sibling, None),
    }

    def when(condition, action):
        if condition is None:
            action()
        else:
            pl.when(condition)(action)

    def both(a, b):
        if a is None:
            return b
        return a if b is None else jnp.logical_and(a, b)

    def region(chunk, source):
        if chunk == chunk_count:
            return pool_ref.at[pl.ds(pl.multiple_of(source * TILE_ROWS, TILE_ROWS), TILE_ROWS), :]
        return buffers[chunk].at[pl.ds(source * local_cubes, local_cubes)]

    used = [0] * (chunk_count + 1)
    sent = []

    def forward(chunk, source, condition, ways):
        for way in ways:
            partner, exists = partners[way]
            slot = used[chunk]
            used[chunk] += 1
            holds = both(condition, exists)
            copy = functools.partial(
                pltpu.make_async_remote_copy,
                send_sem=send_sem.at[chunk, slot],
                recv_sem=recv_sem.at[chunk, source],
                device_id={"cubes": partner},
                device_id_type=pl.DeviceIdType.MESH,
            )

            def start(copy=copy):
                copy(region(chunk, source), region(chunk, source)).start()

            def finish(copy=copy):
                copy(region(chunk, source), region(chunk, source)).wait_send()

            when(holds, start)
            sent.append((holds, finish))

    def arrive(chunk, source, condition):
        def take():
            pltpu.make_async_remote_copy(
                src_ref=region(chunk, source),
                dst_ref=region(chunk, source),
                send_sem=send_sem.at[chunk, 0],
                recv_sem=recv_sem.at[chunk, source],
                device_id={"cubes": sibling},
                device_id_type=pl.DeviceIdType.MESH,
            ).wait_recv()

        when(condition, take)

    def fill(chunk):
        columns = slice(chunk * width, (chunk + 1) * width)
        for cube in range(local_cubes):
            rows = slice(cube * CUBE, (cube + 1) * CUBE)
            buffers[chunk][me * local_cubes + cube, 0] = key_ref[rows, columns]
            buffers[chunk][me * local_cubes + cube, 1] = value_ref[rows, columns]

    parts = TILE_ROWS // (2 * local_cubes)
    part_heads = head_count // parts
    part_width = part_heads * head_size

    def fill_pool():
        rows = []
        for part in range(parts):
            columns = slice(part * part_width, (part + 1) * part_width)
            for ref in (key_ref, value_ref):
                for cube in range(local_cubes):
                    block = ref[cube * CUBE : (cube + 1) * CUBE, columns].astype(jnp.float32)
                    rows.append(jnp.sum(block, axis=0, keepdims=True) * (1.0 / CUBE))
        pool_ref[pl.ds(pl.multiple_of(me * TILE_ROWS, TILE_ROWS), TILE_ROWS), :] = jnp.concatenate(
            rows, axis=0
        ).astype(jnp.bfloat16)

    def compute(chunk):
        buffer = buffers[chunk]

        def one_head(inner, carry):
            head = chunk * chunk_heads + inner
            columns = pl.ds(pl.multiple_of(inner * head_size, head_size), head_size)
            head_columns = pl.ds(pl.multiple_of(head * head_size, head_size), head_size)
            part = head // part_heads
            pool_columns = pl.ds(
                pl.multiple_of((head % part_heads) * head_size, head_size), head_size
            )
            queries = query_ref[:, head_columns]
            pooled = pool_ref[:, pool_columns]
            scores = (
                lax.dot_general(
                    queries, pooled, (((1,), (1,)), ((), ())), preferred_element_type=jnp.float32
                )
                * factor
            )
            row = lax.broadcasted_iota(jnp.int32, scores.shape, 1) & (TILE_ROWS - 1)
            first = part * (2 * local_cubes)
            valid = (row >= first) & (row < first + local_cubes)
            scores = jnp.where(valid, scores, -jnp.inf)
            weights = jnp.exp(scores - jnp.max(scores, axis=1, keepdims=True))
            total = jnp.sum(weights, axis=1, keepdims=True)
            moved = pltpu.roll(weights, local_cubes, 1).astype(jnp.bfloat16)
            coarse = jnp.dot(moved, pooled, preferred_element_type=jnp.float32) / total
            gates = gate_ref[...].astype(jnp.float32)
            lane = lax.broadcasted_iota(jnp.int32, gates.shape, 1)
            coarse_gate = jax.nn.sigmoid(
                jnp.sum(jnp.where(lane == head, gates, 0.0), axis=1, keepdims=True)
            )
            fine_gate = jax.nn.sigmoid(
                jnp.sum(jnp.where(lane == head + head_count, gates, 0.0), axis=1, keepdims=True)
            )
            fine = []
            for cube in range(local_cubes):
                base = (cube * head_count + head) * picks
                chosen = [target_ref[base + pick] for pick in range(picks)]
                keys = jnp.concatenate([buffer[t, 0, :, columns] for t in chosen], axis=0)
                values = jnp.concatenate([buffer[t, 1, :, columns] for t in chosen], axis=0)
                scores = (
                    lax.dot_general(
                        queries[cube * CUBE : (cube + 1) * CUBE],
                        keys,
                        (((1,), (1,)), ((), ())),
                        preferred_element_type=jnp.float32,
                    )
                    * factor
                )
                weights = jnp.exp(scores - jnp.max(scores, axis=1, keepdims=True))
                total = jnp.sum(weights, axis=1, keepdims=True)
                fine.append(
                    jnp.dot(
                        weights.astype(jnp.bfloat16), values, preferred_element_type=jnp.float32
                    )
                    / total
                )
            fine = jnp.concatenate(fine, axis=0)
            out_ref[:, head_columns] = (coarse_gate * coarse + fine_gate * fine).astype(
                out_ref.dtype
            )
            return carry

        lax.fori_loop(0, chunk_heads, one_head, 0)

    events = []
    hop = 0.7

    def add(key, action):
        events.append((key, len(events), action))

    def own(chunk):
        if chunk < chunk_count:
            fill(chunk)
        forward(chunk, me, None, ("up", "down", "across", "sibling"))

    def passing(chunk, source, condition, ways):
        arrive(chunk, source, condition)
        forward(chunk, source, condition, ways)

    def plan(chunk, time, crosses_first):
        add(time - LOOKAHEAD, lambda: own(chunk))
        other = me + CORES * (1 - 2 * x)
        if crosses_first:
            add(time - 0.5, lambda: passing(chunk, other, None, ("up", "down", "sibling")))
        else:
            add(time + 0.1, lambda: passing(chunk, other, None, ("sibling",)))
        for distance in range(1, z_extent):
            for way, source_step, condition in (
                ("up", -distance, z >= distance),
                ("down", distance, z < z_extent - distance),
            ):
                near = me + source_step * z_stride
                far = other + source_step * z_stride
                key = time + hop * (distance - 1)
                if crosses_first:
                    add(key, functools.partial(passing, chunk, near, condition, (way, "sibling")))
                    add(
                        key + 0.3,
                        functools.partial(passing, chunk, far, condition, (way, "sibling")),
                    )
                else:
                    add(
                        key,
                        functools.partial(passing, chunk, near, condition, (way, "across", "sibling")),
                    )
                    add(
                        key + 1.0, functools.partial(passing, chunk, far, condition, ("sibling",))
                    )

        def complete():
            for place in range(z_extent * x_extent):
                arrive(chunk, place * CORES + (1 - core), None)
            if chunk < chunk_count:
                compute(chunk)

        add(time + (z_extent - 2) * hop + 1.1, complete)

    plan(chunk_count, -1.0, False)
    for chunk in range(chunk_count):
        plan(chunk, float(chunk), chunk in x_first)

    barrier = pltpu.get_barrier_semaphore()
    for partner, exists in partners.values():

        def greet(partner=partner):
            pl.semaphore_signal(
                barrier, inc=1, device_id={"cubes": partner}, device_id_type=pl.DeviceIdType.MESH
            )

        when(exists, greet)
    fill_pool()
    pl.semaphore_wait(barrier, 2 + has_up.astype(jnp.int32) + has_down.astype(jnp.int32))
    for key, order, action in sorted(events, key=lambda event: event[:2]):
        action()
    for holds, finish in sent:
        when(holds, finish)


def gathered_body(query_rows, key_rows, value_rows, gate_logits, selection, cube_ids):
    device_count = lax.axis_size("cubes")
    token_count, feature_width = query_rows.shape
    head_count = gate_logits.shape[1] // 2
    head_size = feature_width // head_count
    local_cubes = token_count // CUBE
    total_cubes = cube_ids.shape[0]
    picks = selection.shape[2]
    self_index = lax.axis_index("cubes")
    chosen = lax.dynamic_slice_in_dim(selection, self_index * local_cubes, local_cubes, 0)
    cube_range = jnp.arange(total_cubes, dtype=jnp.int32)
    targets = jnp.sum(
        jnp.where(chosen.reshape(-1)[:, None] == cube_ids[None, :], cube_range[None, :], 0), axis=1
    )
    chunk_heads, chunk_count, unused = head_chunks(head_count)
    width = chunk_heads * head_size
    z_extent, x_extent = grid_of(device_count)
    sends = 4 + 3 * 4 * (z_extent - 1) + 3
    pool_width = head_count * head_size * 2 * local_cubes // TILE_ROWS
    sizes = (device_count, head_count, head_size, local_cubes, picks)
    return pl.pallas_call(
        functools.partial(attention_kernel, sizes),
        out_shape=jax.ShapeDtypeStruct((token_count, feature_width), jnp.bfloat16),
        in_specs=[pl.BlockSpec(memory_space=pltpu.SMEM)]
        + [pl.BlockSpec(memory_space=pltpu.VMEM)] * 4,
        out_specs=pl.BlockSpec(memory_space=pltpu.VMEM),
        scratch_shapes=[
            pltpu.VMEM((total_cubes, 2, CUBE, width), jnp.bfloat16) for unused in range(chunk_count)
        ]
        + [
            pltpu.VMEM((device_count * TILE_ROWS, pool_width), jnp.bfloat16),
            pltpu.SemaphoreType.DMA((chunk_count + 1, sends)),
            pltpu.SemaphoreType.DMA((chunk_count + 1, device_count)),
        ],
        compiler_params=pltpu.CompilerParams(
            collective_id=0, has_side_effects=True, vmem_limit_bytes=VMEM_BUDGET
        ),
    )(targets, query_rows, key_rows, value_rows, gate_logits)


def body(query_rows, key_rows, value_rows, gate_logits, selection, cube_ids):
    device_count = lax.axis_size("cubes")
    token_count, feature_width = query_rows.shape
    head_count = gate_logits.shape[1] // 2
    local_cubes = token_count // CUBE
    gathered_bytes = 2 * device_count * token_count * feature_width * key_rows.dtype.itemsize
    fits = (
        2 * gathered_bytes // 3 <= VMEM_BUDGET // 2
        and device_count % CORES == 0
        and grid_of(device_count)[1] == 2
        and TILE_ROWS % (2 * local_cubes) == 0
        and head_count % (TILE_ROWS // (2 * local_cubes)) == 0
    )
    return (gathered_body if fits else streamed_body)(
        query_rows, key_rows, value_rows, gate_logits, selection, cube_ids
    )


def solution(mesh):
    placed = (
        P(("groups", "cubes"), None),
        P(("groups", "cubes"), None),
        P(("groups", "cubes"), None),
        P(("groups", "cubes"), None),
        P("groups", None, None),
        P("groups"),
    )
    return jax.shard_map(
        body, mesh=mesh, in_specs=placed, out_specs=P(("groups", "cubes"), None), check_vma=False
    )
```

```python
import functools
import math

import jax
import jax.numpy as jnp
from jax import lax
from jax.experimental import pallas as pl
from jax.experimental.pallas import tpu as pltpu
from jax.sharding import PartitionSpec as P

CUBE = 64
HEADS_PER_CHUNK = 2
LOOKAHEAD = 3
SLACK = 0.5


def X_FIRST(chunk_count):
    return (chunk_count // 2 - 1, chunk_count - 1)


NEG_START = -1e30


def block_partials(query_slots, pair_slots):
    head_size = query_slots.shape[-1]
    factor = 1.0 / math.sqrt(head_size)
    slot_keys = pair_slots[:, :, :head_size]
    slot_values = pair_slots[:, :, head_size:]
    scores = (
        jnp.einsum("sqd,skd->sqk", query_slots, slot_keys, preferred_element_type=jnp.float32)
        * factor
    )
    slot_max = jnp.max(scores, axis=2)
    weights = jnp.exp(scores - slot_max[:, :, None])
    slot_total = jnp.sum(weights, axis=2)
    numerator = jnp.einsum(
        "sqk,skd->sqd",
        weights.astype(jnp.bfloat16),
        slot_values,
        preferred_element_type=jnp.float32,
    )
    return (numerator, slot_max, slot_total)


def merge_slots(state, results, slot_group):
    numerator, running_max, totals = state
    slot_numerator, slot_max, slot_total = results
    group_count = numerator.shape[0]
    slot_count = slot_group.shape[0]
    member = slot_group[:, None] == jnp.arange(group_count, dtype=jnp.int32)[None, :]
    is_valid = slot_group >= 0
    group_max = jnp.max(jnp.where(member[:, :, None], slot_max[:, None, :], -jnp.inf), axis=0)
    new_max = jnp.maximum(running_max, group_max)
    slot_base = jnp.take(new_max, jnp.maximum(slot_group, 0), axis=0)
    slot_weight = jnp.exp(jnp.where(is_valid[:, None], slot_max - slot_base, -jnp.inf))
    onehot = member.astype(jnp.float32).T
    weighted = (slot_weight[:, :, None] * slot_numerator).reshape(slot_count, -1)
    added_numerator = jnp.dot(onehot, weighted, precision=lax.Precision.HIGHEST).reshape(
        numerator.shape
    )
    added_total = jnp.dot(onehot, slot_weight * slot_total, precision=lax.Precision.HIGHEST)
    decay_factor = jnp.exp(running_max - new_max)
    return (
        numerator * decay_factor[:, :, None] + added_numerator,
        new_max,
        totals * decay_factor + added_total,
    )


def streamed_body(query_rows, key_rows, value_rows, gate_logits, selection, cube_ids):
    device_count = lax.axis_size("cubes")
    token_count = query_rows.shape[0]
    feature_width = query_rows.shape[1]
    head_count = gate_logits.shape[1] // 2
    head_size = feature_width // head_count
    local_cubes = token_count // CUBE
    total_cubes = cube_ids.shape[0]
    picks_each = selection.shape[2]
    depth_rounds = max(2, head_count * picks_each // device_count + 1)
    request_count = local_cubes * head_count * picks_each
    factor = 1.0 / math.sqrt(head_size)
    self_index = lax.axis_index("cubes")
    pooled_keys = jnp.mean(
        key_rows.reshape(local_cubes, CUBE, feature_width), axis=1, dtype=jnp.float32
    ).astype(jnp.bfloat16)
    pooled_values = jnp.mean(
        value_rows.reshape(local_cubes, CUBE, feature_width), axis=1, dtype=jnp.float32
    ).astype(jnp.bfloat16)
    query_heads = query_rows.reshape(token_count, head_count, head_size)
    start_state = (
        jnp.zeros((head_count, token_count, head_size), jnp.float32),
        jnp.full((head_count, token_count), NEG_START, jnp.float32),
        jnp.zeros((head_count, token_count), jnp.float32),
    )
    numerator, running_max, totals = start_state
    piece_keys = lax.all_gather(pooled_keys, "cubes", axis=0, tiled=True)
    piece_values = lax.all_gather(pooled_values, "cubes", axis=0, tiled=True)
    piece_rows = piece_keys.shape[0]
    scores = (
        jnp.einsum(
            "thd,jhd->htj",
            query_heads,
            piece_keys.reshape(piece_rows, head_count, head_size),
            preferred_element_type=jnp.float32,
        )
        * factor
    )
    new_max = jnp.maximum(running_max, jnp.max(scores, axis=2))
    weights = jnp.exp(scores - new_max[:, :, None])
    added = jnp.einsum(
        "htj,jhd->htd",
        weights.astype(jnp.bfloat16),
        piece_values.reshape(piece_rows, head_count, head_size),
        preferred_element_type=jnp.float32,
    )
    numerator = added
    totals = jnp.sum(weights, axis=2)
    coarse = jnp.transpose(numerator / totals[:, :, None], (1, 0, 2))
    cube_range = jnp.arange(total_cubes, dtype=jnp.int32)
    position = jnp.sum(
        jnp.where(cube_ids[None, :] == cube_range[:, None], cube_range[None, :], 0), axis=1
    )
    targets = jnp.take(position, selection.reshape(-1)).reshape(device_count, request_count)
    request_range = jnp.arange(request_count, dtype=jnp.int32)
    request_group = request_range // picks_each
    request_head = request_group % head_count
    round_range = jnp.arange(depth_rounds, dtype=jnp.int32)
    own_targets = lax.dynamic_index_in_dim(targets, self_index, 0, keepdims=False)
    same_target = own_targets[:, None] == cube_range[None, :]
    running_count = jnp.cumsum(same_target.astype(jnp.int32), axis=0)
    own_rank = jnp.sum(jnp.where(same_target, running_count, 0), axis=1) - 1
    chosen_round = same_target[None, :, :] & (own_rank[None, :, None] == round_range[:, None, None])
    wanted_all = jnp.sum(jnp.where(chosen_round, request_group[None, :, None] + 1, 0), axis=1) - 1
    own_cubes = self_index * local_cubes + jnp.arange(local_cubes, dtype=jnp.int32)
    hit_mine = targets[:, :, None] == own_cubes[None, None, :]
    mine_rank = jnp.cumsum(hit_mine.astype(jnp.int32), axis=1) - 1
    round_hit = hit_mine[None] & (mine_rank[None] == round_range[:, None, None, None])
    incoming_all = (
        jnp.sum(jnp.where(round_hit, request_head[None, None, :, None] + 1, 0), axis=2) - 1
    )
    query_groups = (
        query_rows.reshape(local_cubes, CUBE, head_count, head_size)
        .transpose(0, 2, 1, 3)
        .reshape(local_cubes * head_count, CUBE, head_size)
    )
    pair_blocks = jnp.concatenate(
        (
            key_rows.reshape(local_cubes, CUBE, head_count, head_size),
            value_rows.reshape(local_cubes, CUBE, head_count, head_size),
        ),
        axis=3,
    )
    pair_groups = pair_blocks.transpose(0, 2, 1, 3).reshape(
        local_cubes * head_count, CUBE, 2 * head_size
    )
    base_group = head_count * jnp.arange(local_cubes, dtype=jnp.int32)

    def held_pairs(incoming):
        source = (jnp.maximum(incoming, 0) + base_group[None, :]).reshape(-1)
        picked = jnp.take(pair_groups, source, axis=0)
        return jnp.where(
            (incoming >= 0).reshape(-1)[:, None, None], picked, jnp.zeros((), jnp.bfloat16)
        )

    def asked_queries(wanted):
        picked = jnp.take(query_groups, jnp.maximum(wanted, 0), axis=0)
        return jnp.where((wanted >= 0)[:, None, None], picked, jnp.zeros((), jnp.bfloat16))

    def one_round(state, tables):
        wanted, incoming = tables
        arrived = lax.all_to_all(
            held_pairs(incoming), "cubes", split_axis=0, concat_axis=0, tiled=True
        )
        results = block_partials(asked_queries(wanted), arrived)
        return (merge_slots(state, results, wanted), None)

    group_count = local_cubes * head_count
    start_state = (
        jnp.zeros((group_count, CUBE, head_size), jnp.float32),
        jnp.full((group_count, CUBE), NEG_START, jnp.float32),
        jnp.zeros((group_count, CUBE), jnp.float32),
    )
    final_state, unused = lax.scan(one_round, start_state, (wanted_all, incoming_all))
    numerator, running_max, totals = final_state
    fine_groups = numerator / totals[:, :, None]
    fine = (
        fine_groups.reshape(local_cubes, head_count, CUBE, head_size)
        .transpose(0, 2, 1, 3)
        .reshape(token_count, head_count, head_size)
    )
    gates = jax.nn.sigmoid(gate_logits.astype(jnp.float32))
    mixed = gates[:, :head_count, None] * coarse + gates[:, head_count:, None] * fine
    return mixed.reshape(token_count, feature_width).astype(jnp.bfloat16)

CORES = 2
TILE_ROWS = 16
VMEM_BUDGET = 40 * 1024 * 1024
VMEM_GRANT = 62 * 1024 * 1024


def grid_of(device_count):
    chips = device_count // CORES
    x_extent = 1
    for extent in range(1, chips + 1):
        if chips % extent == 0 and extent**3 <= chips:
            x_extent = extent
    return (chips // x_extent, x_extent)


def head_chunks(head_count):
    chunk_heads = HEADS_PER_CHUNK if head_count % HEADS_PER_CHUNK == 0 else 1
    chunk_count = head_count // chunk_heads
    return (chunk_heads, chunk_count, set(X_FIRST(chunk_count)))


def attention_kernel(
    sizes, target_ref, query_rows, key_cubes, value_cubes, gate_rows, out_ref, *scratch
):
    device_count, head_count, head_size, local_cubes, picks = sizes
    chunk_heads, chunk_count, x_first = head_chunks(head_count)
    z_extent, x_extent = grid_of(device_count)
    buffers = scratch[:chunk_count]
    pool_ref = scratch[chunk_count]
    query_ref, gate_ref, send_sem, recv_sem, local_sem = scratch[chunk_count + 1 :]
    width = chunk_heads * head_size
    factor = 1.0 / math.sqrt(head_size)
    z_stride = x_extent * CORES
    me = lax.axis_index("cubes")
    z = me // z_stride
    x = (me // CORES) % x_extent
    core = me % CORES
    sibling = me + 1 - 2 * core
    across = me + CORES * (1 - 2 * x)
    has_up = z < z_extent - 1
    has_down = z > 0
    partners = {
        "up": (me + z_stride, has_up),
        "down": (me - z_stride, has_down),
        "across": (across, None),
        "sibling": (sibling, None),
    }

    def when(condition, action):
        if condition is None:
            action()
        else:
            pl.when(condition)(action)

    def both(a, b):
        if a is None:
            return b
        return a if b is None else jnp.logical_and(a, b)

    def region(chunk, source):
        if chunk == chunk_count:
            return pool_ref.at[pl.ds(pl.multiple_of(source * TILE_ROWS, TILE_ROWS), TILE_ROWS), :]
        return buffers[chunk].at[pl.ds(source * local_cubes, local_cubes)]

    slots = {}
    sent = []

    def forward(chunk, source, condition, ways, name):
        for way in ways:
            partner, exists = partners[way]
            turn = "z" if way in ("up", "down") and name[0] in ("near", "far") else way
            slot = slots.setdefault((chunk, name, turn), sum(key[0] == chunk for key in slots))
            holds = both(condition, exists)
            copy = functools.partial(
                pltpu.make_async_remote_copy,
                send_sem=send_sem.at[chunk, slot],
                recv_sem=recv_sem.at[chunk, source],
                device_id={"cubes": partner},
                device_id_type=pl.DeviceIdType.MESH,
            )

            def start(copy=copy):
                copy(region(chunk, source), region(chunk, source)).start()

            def finish(copy=copy):
                copy(region(chunk, source), region(chunk, source)).wait_send()

            when(holds, start)
            sent.append((holds, finish))

    def arrive(chunk, source, condition):
        def take():
            pltpu.make_async_remote_copy(
                src_ref=region(chunk, source),
                dst_ref=region(chunk, source),
                send_sem=send_sem.at[chunk, 0],
                recv_sem=recv_sem.at[chunk, source],
                device_id={"cubes": sibling},
                device_id_type=pl.DeviceIdType.MESH,
            ).wait_recv()

        when(condition, take)

    def fills(chunk):
        columns = pl.ds(chunk * width, width)
        mine = pl.ds(me * local_cubes, local_cubes)
        return [
            pltpu.make_async_copy(
                ref.at[:, :, columns], buffers[chunk].at[mine, kind], local_sem.at[chunk, kind]
            )
            for kind, ref in enumerate((key_cubes, value_cubes))
        ]

    def query_fills():
        return [
            pltpu.make_async_copy(query_rows, query_ref, local_sem.at[chunk_count, 0]),
            pltpu.make_async_copy(gate_rows, gate_ref, local_sem.at[chunk_count, 1]),
        ]

    parts = TILE_ROWS // (2 * local_cubes)
    part_heads = head_count // parts

    def fill_pool():
        def mean_row(head, kind, cube):
            start = (head % chunk_heads) * head_size
            buffer = buffers[head // chunk_heads]
            block = buffer[me * local_cubes + cube, kind, :, start : start + head_size]
            return jnp.sum(block.astype(jnp.float32), axis=0, keepdims=True) * (1.0 / CUBE)

        rows = []
        for part in range(parts):
            heads = range(part * part_heads, (part + 1) * part_heads)
            for kind in range(2):
                for cube in range(local_cubes):
                    rows.append(
                        jnp.concatenate([mean_row(head, kind, cube) for head in heads], axis=1)
                    )
        pool_ref[pl.ds(pl.multiple_of(me * TILE_ROWS, TILE_ROWS), TILE_ROWS), :] = jnp.concatenate(
            rows, axis=0
        ).astype(jnp.bfloat16)

    def compute(chunk, inner):
        buffer = buffers[chunk]

        def one_head():
            head = chunk * chunk_heads + inner
            columns = pl.ds(pl.multiple_of(inner * head_size, head_size), head_size)
            head_columns = pl.ds(pl.multiple_of(head * head_size, head_size), head_size)
            part = head // part_heads
            pool_columns = pl.ds(
                pl.multiple_of((head % part_heads) * head_size, head_size), head_size
            )
            queries = query_ref[:, head_columns]
            pooled = pool_ref[:, pool_columns]
            scores = (
                lax.dot_general(
                    queries, pooled, (((1,), (1,)), ((), ())), preferred_element_type=jnp.float32
                )
                * factor
            )
            row = lax.broadcasted_iota(jnp.int32, scores.shape, 1) & (TILE_ROWS - 1)
            first = part * (2 * local_cubes)
            valid = (row >= first) & (row < first + local_cubes)
            scores = jnp.where(valid, scores, -jnp.inf)
            weights = jnp.exp(scores - jnp.max(scores, axis=1, keepdims=True))
            total = jnp.sum(weights, axis=1, keepdims=True)
            moved = pltpu.roll(weights, local_cubes, 1).astype(jnp.bfloat16)
            coarse = jnp.dot(moved, pooled, preferred_element_type=jnp.float32) / total
            gates = gate_ref[...].astype(jnp.float32)
            lane = lax.broadcasted_iota(jnp.int32, gates.shape, 1)
            coarse_gate = jax.nn.sigmoid(
                jnp.sum(jnp.where(lane == head, gates, 0.0), axis=1, keepdims=True)
            )
            fine_gate = jax.nn.sigmoid(
                jnp.sum(jnp.where(lane == head + head_count, gates, 0.0), axis=1, keepdims=True)
            )
            fine = []
            for cube in range(local_cubes):
                base = (cube * head_count + head) * picks
                chosen = [target_ref[base + pick] for pick in range(picks)]
                keys = jnp.concatenate([buffer[t, 0, :, columns] for t in chosen], axis=0)
                values = jnp.concatenate([buffer[t, 1, :, columns] for t in chosen], axis=0)
                scores = (
                    lax.dot_general(
                        queries[cube * CUBE : (cube + 1) * CUBE],
                        keys,
                        (((1,), (1,)), ((), ())),
                        preferred_element_type=jnp.float32,
                    )
                    * factor
                )
                weights = jnp.exp(scores - jnp.max(scores, axis=1, keepdims=True))
                total = jnp.sum(weights, axis=1, keepdims=True)
                fine.append(
                    jnp.dot(
                        weights.astype(jnp.bfloat16), values, preferred_element_type=jnp.float32
                    )
                    / total
                )
            fine = jnp.concatenate(fine, axis=0)
            out_ref[:, head_columns] = (coarse_gate * coarse + fine_gate * fine).astype(
                out_ref.dtype
            )

        one_head()

    events = []
    hop = 0.7

    def add(key, action):
        events.append((key, len(events), action))

    filled = set()

    def own(chunk):
        for needed in range(chunk_count) if chunk == chunk_count else (chunk,):
            if needed not in filled:
                filled.add(needed)
                for copy in fills(needed):
                    copy.wait()
        if chunk == chunk_count:
            fill_pool()
        forward(chunk, me, None, ("up", "down", "across", "sibling"), ("own", 0))

    def passing(chunk, source, condition, ways, name):
        arrive(chunk, source, condition)
        forward(chunk, source, condition, ways, name)

    def plan(chunk, time, crosses_first, own_time):
        add(own_time, lambda: own(chunk))
        other = me + CORES * (1 - 2 * x)
        if crosses_first:
            add(time - 0.5, lambda: passing(chunk, other, None, ("up", "down", "sibling"), ("other", 0)))
        else:
            add(time + 0.1, lambda: passing(chunk, other, None, ("sibling",), ("other", 0)))
        for distance in range(1, z_extent):
            for way, source_step, condition in (
                ("up", -distance, z >= distance),
                ("down", distance, z < z_extent - distance),
            ):
                near = me + source_step * z_stride
                far = other + source_step * z_stride
                key = time + hop * (distance - 1)
                turn = distance if way == "up" else z_extent - distance
                onward = (way, "sibling") if crosses_first else (way, "across", "sibling")
                far_onward = (way, "sibling") if crosses_first else ("sibling",)
                far_key = key + (0.3 if crosses_first else 1.0)
                for moment, source, ways, name in (
                    (key, near, onward, ("near", turn)),
                    (far_key, far, far_onward, ("far", turn)),
                ):
                    add(moment, functools.partial(passing, chunk, source, condition, ways, name))

        def complete():
            for place in range(z_extent * x_extent):
                arrive(chunk, place * CORES + (1 - core), None)

        end = time + (z_extent - 2) * hop + 1.1
        if chunk == chunk_count:
            add(end, complete)
            return
        add(end + SLACK, complete)
        for inner in range(chunk_heads):
            add(end + SLACK + inner / chunk_heads, functools.partial(compute, chunk, inner))

    plan(chunk_count, 0.3, False, -0.9)
    for chunk in range(chunk_count):
        plan(chunk, float(chunk), chunk in x_first, float(chunk - LOOKAHEAD))

    for chunk in range(chunk_count):
        for copy in fills(chunk):
            copy.start()
    for copy in query_fills():
        copy.start()
    barrier = pltpu.get_barrier_semaphore()
    for partner, exists in partners.values():

        def greet(partner=partner):
            pl.semaphore_signal(
                barrier, inc=1, device_id={"cubes": partner}, device_id_type=pl.DeviceIdType.MESH
            )

        when(exists, greet)
    pl.semaphore_wait(barrier, 2 + has_up.astype(jnp.int32) + has_down.astype(jnp.int32))
    for copy in query_fills():
        copy.wait()
    for key, order, action in sorted(events, key=lambda event: event[:2]):
        action()
    for holds, finish in sent:
        when(holds, finish)


def gathered_body(query_rows, key_rows, value_rows, gate_logits, selection, cube_ids):
    device_count = lax.axis_size("cubes")
    token_count, feature_width = query_rows.shape
    head_count = gate_logits.shape[1] // 2
    head_size = feature_width // head_count
    local_cubes = token_count // CUBE
    total_cubes = cube_ids.shape[0]
    picks = selection.shape[2]
    self_index = lax.axis_index("cubes")
    chosen = lax.dynamic_slice_in_dim(selection, self_index * local_cubes, local_cubes, 0)
    cube_range = jnp.arange(total_cubes, dtype=jnp.int32)
    targets = jnp.sum(
        jnp.where(chosen.reshape(-1)[:, None] == cube_ids[None, :], cube_range[None, :], 0), axis=1
    )
    chunk_heads, chunk_count, unused = head_chunks(head_count)
    width = chunk_heads * head_size
    z_extent, x_extent = grid_of(device_count)
    sends = 4 + 3 + 4 * (z_extent - 1)
    pool_width = head_count * head_size * 2 * local_cubes // TILE_ROWS
    sizes = (device_count, head_count, head_size, local_cubes, picks)
    return pl.pallas_call(
        functools.partial(attention_kernel, sizes),
        out_shape=jax.ShapeDtypeStruct((token_count, feature_width), jnp.bfloat16),
        in_specs=[pl.BlockSpec(memory_space=pltpu.SMEM)]
        + [pl.BlockSpec(memory_space=pltpu.HBM)] * 4,
        out_specs=pl.BlockSpec(memory_space=pltpu.VMEM),
        scratch_shapes=[
            pltpu.VMEM((total_cubes, 2, CUBE, width), jnp.bfloat16) for unused in range(chunk_count)
        ]
        + [
            pltpu.VMEM((device_count * TILE_ROWS, pool_width), jnp.bfloat16),
            pltpu.VMEM(query_rows.shape, query_rows.dtype),
            pltpu.VMEM(gate_logits.shape, gate_logits.dtype),
            pltpu.SemaphoreType.DMA((chunk_count + 1, sends)),
            pltpu.SemaphoreType.DMA((chunk_count + 1, device_count)),
            pltpu.SemaphoreType.DMA((chunk_count + 1, 2)),
        ],
        compiler_params=pltpu.CompilerParams(
            collective_id=0, has_side_effects=True, vmem_limit_bytes=VMEM_GRANT
        ),
    )(
        targets,
        query_rows,
        key_rows.reshape(local_cubes, CUBE, feature_width),
        value_rows.reshape(local_cubes, CUBE, feature_width),
        gate_logits,
    )


def body(query_rows, key_rows, value_rows, gate_logits, selection, cube_ids):
    device_count = lax.axis_size("cubes")
    token_count, feature_width = query_rows.shape
    head_count = gate_logits.shape[1] // 2
    local_cubes = token_count // CUBE
    gathered_bytes = 2 * device_count * token_count * feature_width * key_rows.dtype.itemsize
    fits = (
        2 * gathered_bytes // 3 <= VMEM_BUDGET // 2
        and device_count % CORES == 0
        and grid_of(device_count)[1] == 2
        and TILE_ROWS % (2 * local_cubes) == 0
        and head_count % (TILE_ROWS // (2 * local_cubes)) == 0
    )
    return (gathered_body if fits else streamed_body)(
        query_rows, key_rows, value_rows, gate_logits, selection, cube_ids
    )


def solution(mesh):
    placed = (
        P(("groups", "cubes"), None),
        P(("groups", "cubes"), None),
        P(("groups", "cubes"), None),
        P(("groups", "cubes"), None),
        P("groups", None, None),
        P("groups"),
    )
    return jax.shard_map(
        body, mesh=mesh, in_specs=placed, out_specs=P(("groups", "cubes"), None), check_vma=False
    )
```

```python
import functools
import math

import jax
import jax.numpy as jnp
from jax import lax
from jax.experimental import pallas as pl
from jax.experimental.pallas import tpu as pltpu
from jax.sharding import PartitionSpec as P

CUBE = 64
LOOKAHEAD = 2


NEG_START = -1e30


def block_partials(query_slots, pair_slots):
    head_size = query_slots.shape[-1]
    factor = 1.0 / math.sqrt(head_size)
    slot_keys = pair_slots[:, :, :head_size]
    slot_values = pair_slots[:, :, head_size:]
    scores = (
        jnp.einsum("sqd,skd->sqk", query_slots, slot_keys, preferred_element_type=jnp.float32)
        * factor
    )
    slot_max = jnp.max(scores, axis=2)
    weights = jnp.exp(scores - slot_max[:, :, None])
    slot_total = jnp.sum(weights, axis=2)
    numerator = jnp.einsum(
        "sqk,skd->sqd",
        weights.astype(jnp.bfloat16),
        slot_values,
        preferred_element_type=jnp.float32,
    )
    return (numerator, slot_max, slot_total)


def merge_slots(state, results, slot_group):
    numerator, running_max, totals = state
    slot_numerator, slot_max, slot_total = results
    group_count = numerator.shape[0]
    slot_count = slot_group.shape[0]
    member = slot_group[:, None] == jnp.arange(group_count, dtype=jnp.int32)[None, :]
    is_valid = slot_group >= 0
    group_max = jnp.max(jnp.where(member[:, :, None], slot_max[:, None, :], -jnp.inf), axis=0)
    new_max = jnp.maximum(running_max, group_max)
    slot_base = jnp.take(new_max, jnp.maximum(slot_group, 0), axis=0)
    slot_weight = jnp.exp(jnp.where(is_valid[:, None], slot_max - slot_base, -jnp.inf))
    onehot = member.astype(jnp.float32).T
    weighted = (slot_weight[:, :, None] * slot_numerator).reshape(slot_count, -1)
    added_numerator = jnp.dot(onehot, weighted, precision=lax.Precision.HIGHEST).reshape(
        numerator.shape
    )
    added_total = jnp.dot(onehot, slot_weight * slot_total, precision=lax.Precision.HIGHEST)
    decay_factor = jnp.exp(running_max - new_max)
    return (
        numerator * decay_factor[:, :, None] + added_numerator,
        new_max,
        totals * decay_factor + added_total,
    )


def streamed_body(query_rows, key_rows, value_rows, gate_logits, selection, cube_ids):
    device_count = lax.axis_size("cubes")
    token_count = query_rows.shape[0]
    feature_width = query_rows.shape[1]
    head_count = gate_logits.shape[1] // 2
    head_size = feature_width // head_count
    local_cubes = token_count // CUBE
    total_cubes = cube_ids.shape[0]
    picks_each = selection.shape[2]
    depth_rounds = max(2, head_count * picks_each // device_count + 1)
    request_count = local_cubes * head_count * picks_each
    factor = 1.0 / math.sqrt(head_size)
    self_index = lax.axis_index("cubes")
    pooled_keys = jnp.mean(
        key_rows.reshape(local_cubes, CUBE, feature_width), axis=1, dtype=jnp.float32
    ).astype(jnp.bfloat16)
    pooled_values = jnp.mean(
        value_rows.reshape(local_cubes, CUBE, feature_width), axis=1, dtype=jnp.float32
    ).astype(jnp.bfloat16)
    query_heads = query_rows.reshape(token_count, head_count, head_size)
    start_state = (
        jnp.zeros((head_count, token_count, head_size), jnp.float32),
        jnp.full((head_count, token_count), NEG_START, jnp.float32),
        jnp.zeros((head_count, token_count), jnp.float32),
    )
    numerator, running_max, totals = start_state
    piece_keys = lax.all_gather(pooled_keys, "cubes", axis=0, tiled=True)
    piece_values = lax.all_gather(pooled_values, "cubes", axis=0, tiled=True)
    piece_rows = piece_keys.shape[0]
    scores = (
        jnp.einsum(
            "thd,jhd->htj",
            query_heads,
            piece_keys.reshape(piece_rows, head_count, head_size),
            preferred_element_type=jnp.float32,
        )
        * factor
    )
    new_max = jnp.maximum(running_max, jnp.max(scores, axis=2))
    weights = jnp.exp(scores - new_max[:, :, None])
    added = jnp.einsum(
        "htj,jhd->htd",
        weights.astype(jnp.bfloat16),
        piece_values.reshape(piece_rows, head_count, head_size),
        preferred_element_type=jnp.float32,
    )
    numerator = added
    totals = jnp.sum(weights, axis=2)
    coarse = jnp.transpose(numerator / totals[:, :, None], (1, 0, 2))
    cube_range = jnp.arange(total_cubes, dtype=jnp.int32)
    position = jnp.sum(
        jnp.where(cube_ids[None, :] == cube_range[:, None], cube_range[None, :], 0), axis=1
    )
    targets = jnp.take(position, selection.reshape(-1)).reshape(device_count, request_count)
    request_range = jnp.arange(request_count, dtype=jnp.int32)
    request_group = request_range // picks_each
    request_head = request_group % head_count
    round_range = jnp.arange(depth_rounds, dtype=jnp.int32)
    own_targets = lax.dynamic_index_in_dim(targets, self_index, 0, keepdims=False)
    same_target = own_targets[:, None] == cube_range[None, :]
    running_count = jnp.cumsum(same_target.astype(jnp.int32), axis=0)
    own_rank = jnp.sum(jnp.where(same_target, running_count, 0), axis=1) - 1
    chosen_round = same_target[None, :, :] & (own_rank[None, :, None] == round_range[:, None, None])
    wanted_all = jnp.sum(jnp.where(chosen_round, request_group[None, :, None] + 1, 0), axis=1) - 1
    own_cubes = self_index * local_cubes + jnp.arange(local_cubes, dtype=jnp.int32)
    hit_mine = targets[:, :, None] == own_cubes[None, None, :]
    mine_rank = jnp.cumsum(hit_mine.astype(jnp.int32), axis=1) - 1
    round_hit = hit_mine[None] & (mine_rank[None] == round_range[:, None, None, None])
    incoming_all = (
        jnp.sum(jnp.where(round_hit, request_head[None, None, :, None] + 1, 0), axis=2) - 1
    )
    query_groups = (
        query_rows.reshape(local_cubes, CUBE, head_count, head_size)
        .transpose(0, 2, 1, 3)
        .reshape(local_cubes * head_count, CUBE, head_size)
    )
    pair_blocks = jnp.concatenate(
        (
            key_rows.reshape(local_cubes, CUBE, head_count, head_size),
            value_rows.reshape(local_cubes, CUBE, head_count, head_size),
        ),
        axis=3,
    )
    pair_groups = pair_blocks.transpose(0, 2, 1, 3).reshape(
        local_cubes * head_count, CUBE, 2 * head_size
    )
    base_group = head_count * jnp.arange(local_cubes, dtype=jnp.int32)

    def held_pairs(incoming):
        source = (jnp.maximum(incoming, 0) + base_group[None, :]).reshape(-1)
        picked = jnp.take(pair_groups, source, axis=0)
        return jnp.where(
            (incoming >= 0).reshape(-1)[:, None, None], picked, jnp.zeros((), jnp.bfloat16)
        )

    def asked_queries(wanted):
        picked = jnp.take(query_groups, jnp.maximum(wanted, 0), axis=0)
        return jnp.where((wanted >= 0)[:, None, None], picked, jnp.zeros((), jnp.bfloat16))

    def one_round(state, tables):
        wanted, incoming = tables
        arrived = lax.all_to_all(
            held_pairs(incoming), "cubes", split_axis=0, concat_axis=0, tiled=True
        )
        results = block_partials(asked_queries(wanted), arrived)
        return (merge_slots(state, results, wanted), None)

    group_count = local_cubes * head_count
    start_state = (
        jnp.zeros((group_count, CUBE, head_size), jnp.float32),
        jnp.full((group_count, CUBE), NEG_START, jnp.float32),
        jnp.zeros((group_count, CUBE), jnp.float32),
    )
    final_state, unused = lax.scan(one_round, start_state, (wanted_all, incoming_all))
    numerator, running_max, totals = final_state
    fine_groups = numerator / totals[:, :, None]
    fine = (
        fine_groups.reshape(local_cubes, head_count, CUBE, head_size)
        .transpose(0, 2, 1, 3)
        .reshape(token_count, head_count, head_size)
    )
    gates = jax.nn.sigmoid(gate_logits.astype(jnp.float32))
    mixed = gates[:, :head_count, None] * coarse + gates[:, head_count:, None] * fine
    return mixed.reshape(token_count, feature_width).astype(jnp.bfloat16)

CORES = 2
HALVES = 2
SITES = 4
VMEM_GRANT = 62 * 1024 * 1024


def grid_of(device_count):
    chips = device_count // CORES
    x_extent = 1
    for extent in range(1, chips + 1):
        if chips % extent == 0 and extent**3 <= chips:
            x_extent = extent
    return (chips // x_extent, x_extent)


def attention_kernel(
    sizes,
    position_ref,
    selection_ref,
    query_rows,
    key_cubes,
    value_cubes,
    gate_rows,
    out_ref,
    *scratch,
):
    head_count, head_size, local_cubes, picks = sizes
    site_heads = head_count // SITES
    buffers = scratch[:site_heads]
    (stage, query_ref, gate_ref, done, out_block) = scratch[site_heads : site_heads + 5]
    (kv_send, kv_recv, query_send, query_recv, out_send, out_recv, kv_local, query_local) = scratch[
        site_heads + 5 :
    ]
    factor = 1.0 / math.sqrt(head_size)
    width = site_heads * head_size
    me = lax.axis_index("cubes")
    core = me % CORES
    x = (me // CORES) % 2
    low = (me // (2 * CORES)) % 2
    half = me // (4 * CORES)
    sibling = me + 1 - 2 * core

    def flip(bit, on):
        return bit + on * (1 - 2 * bit)

    def device(turn):
        return (
            (flip(half, turn // 4) * 2 + flip(low, (turn // 2) % 2)) * 2 + flip(x, turn % 2)
        ) * CORES + core

    def group(turn):
        return flip(x, turn % 2) * 2 + flip(low, (turn // 2) % 2)

    def head_columns(head, count):
        return pl.ds(pl.multiple_of(head * head_size, head_size), count * head_size)

    def cubes_of(source):
        return pl.ds(source * local_cubes, local_cubes)

    def remote(source, target, send, recv, partner):
        return pltpu.make_async_remote_copy(
            src_ref=source,
            dst_ref=target,
            send_sem=send,
            recv_sem=recv,
            device_id={"cubes": partner},
            device_id_type=pl.DeviceIdType.MESH,
        )

    def held(turn, inner):
        if turn % SITES == 0:
            return buffers[inner].at[cubes_of(me)]
        return stage.at[turn % SITES - 1, inner]

    def fills(turn, inner):
        columns = head_columns(group(turn) * site_heads + inner, 1)
        return [
            pltpu.make_async_copy(
                ref.at[:, :, columns], held(turn, inner).at[:, kind], kv_local.at[turn, inner, kind]
            )
            for kind, ref in enumerate((key_cubes, value_cubes))
        ]

    def own_queries():
        columns = head_columns(group(0) * site_heads, site_heads)
        return [
            pltpu.make_async_copy(query_rows.at[:, columns], query_ref.at[0], query_local.at[0]),
            pltpu.make_async_copy(gate_rows, gate_ref.at[0], query_local.at[1]),
        ]

    def query_copies(turn):
        columns = head_columns(group(turn) * site_heads, site_heads)
        return [
            remote(
                query_rows.at[:, columns],
                query_ref.at[turn],
                query_send.at[0, turn],
                query_recv.at[0, turn],
                device(turn),
            ),
            remote(
                gate_ref.at[0],
                gate_ref.at[turn],
                query_send.at[1, turn],
                query_recv.at[1, turn],
                device(turn),
            ),
        ]

    def kv_copy(turn, inner):
        return remote(
            held(turn, inner),
            buffers[inner].at[cubes_of(me)],
            kv_send.at[inner, turn],
            kv_recv.at[inner, turn],
            device(turn),
        )

    def kv_arrival(turn, inner):
        region = buffers[inner].at[cubes_of(device(turn))]
        return remote(
            region, region, kv_send.at[inner, turn], kv_recv.at[inner, turn], device(turn)
        )

    turns = SITES * HALVES

    def pass_on(turn, inner):
        region = buffers[inner].at[cubes_of(device(turn))]
        slot = turns + turn
        return remote(region, region, kv_send.at[inner, slot], kv_recv.at[inner, slot], sibling)

    def passed_arrival(turn, inner):
        region = buffers[inner].at[cubes_of(device(turn) + 1 - 2 * core)]
        slot = turns + turn
        return remote(region, region, kv_send.at[inner, slot], kv_recv.at[inner, slot], sibling)

    def out_copy(turn, inner):
        columns = head_columns(group(0) * site_heads + inner, 1)
        return remote(
            done.at[inner, turn],
            out_block.at[:, columns],
            out_send.at[inner, turn],
            out_recv.at[inner, turn],
            device(turn),
        )

    def out_arrival(turn, inner):
        columns = head_columns(group(turn) * site_heads + inner, 1)
        return remote(
            done.at[inner, turn],
            out_block.at[:, columns],
            out_send.at[inner, turn],
            out_recv.at[inner, turn],
            device(turn),
        )

    def compute(inner):
        buffer = buffers[inner]
        head = group(0) * site_heads + inner
        columns = slice(inner * head_size, (inner + 1) * head_size)

        def pooled(kind):
            cubes = buffer[:, kind].astype(jnp.float32)
            return (jnp.sum(cubes, axis=1) * (1.0 / CUBE)).astype(jnp.bfloat16)

        pooled_keys = pooled(0)
        pooled_values = pooled(1)

        def softmax(queries, keys, values):
            scores = (
                lax.dot_general(
                    queries, keys, (((1,), (1,)), ((), ())), preferred_element_type=jnp.float32
                )
                * factor
            )
            weights = jnp.exp(scores - jnp.max(scores, axis=1, keepdims=True))
            total = jnp.sum(weights, axis=1, keepdims=True)
            return (
                jnp.dot(weights.astype(jnp.bfloat16), values, preferred_element_type=jnp.float32)
                / total
            )

        def one_turn(turn, carry):
            queries = query_ref[turn, :, columns]
            coarse = softmax(queries, pooled_keys, pooled_values)
            gates = gate_ref[turn].astype(jnp.float32)
            lane = lax.broadcasted_iota(jnp.int32, gates.shape, 1)
            coarse_gate = jax.nn.sigmoid(
                jnp.sum(jnp.where(lane == head, gates, 0.0), axis=1, keepdims=True)
            )
            fine_gate = jax.nn.sigmoid(
                jnp.sum(jnp.where(lane == head + head_count, gates, 0.0), axis=1, keepdims=True)
            )
            fine = []
            for cube in range(local_cubes):
                block = device(turn) * local_cubes + cube
                base = (block * head_count + head) * picks
                chosen = [position_ref[selection_ref[base + pick]] for pick in range(picks)]
                keys = jnp.concatenate([buffer[t, 0] for t in chosen], axis=0)
                values = jnp.concatenate([buffer[t, 1] for t in chosen], axis=0)
                fine.append(softmax(queries[cube * CUBE : (cube + 1) * CUBE], keys, values))
            fine = jnp.concatenate(fine, axis=0)
            done[inner, turn] = (coarse_gate * coarse + fine_gate * fine).astype(done.dtype)
            return carry

        lax.fori_loop(0, SITES, one_turn, 0)
        for turn in range(1, SITES):
            out_copy(turn, inner).start()
        out_block[:, head_columns(head, 1)] = done[inner, 0]

    far_first = (7, 6, 5, 4, 3, 2, 1)

    def send(inner):
        for turn in range(SITES):
            for copy in fills(turn, inner):
                copy.wait()
        for turn in far_first:
            kv_copy(turn, inner).start()
        pass_on(0, inner).start()

    for copy in own_queries():
        copy.start()
    for inner in range(site_heads):
        for turn in range(SITES):
            for copy in fills(turn, inner):
                copy.start()
    barrier = pltpu.get_barrier_semaphore()
    for partner in [sibling] + [device(turn) for turn in range(1, turns)]:
        pl.semaphore_signal(
            barrier, inc=1, device_id={"cubes": partner}, device_id_type=pl.DeviceIdType.MESH
        )
    pl.semaphore_wait(barrier, turns)
    for copy in own_queries():
        copy.wait()
    for turn in range(1, SITES):
        for copy in query_copies(turn):
            copy.start()
    for inner in range(min(LOOKAHEAD, site_heads)):
        send(inner)
    for inner in range(site_heads):
        for turn in range(1, turns):
            kv_arrival(turn, inner).wait_recv()
            pass_on(turn, inner).start()
        if inner + LOOKAHEAD < site_heads:
            send(inner + LOOKAHEAD)
        if inner == 0:
            for turn in range(1, SITES):
                for copy in query_copies(turn):
                    copy.wait_recv()
        for turn in range(turns):
            passed_arrival(turn, inner).wait_recv()
        compute(inner)
    for inner in range(site_heads):
        for turn in range(1, SITES):
            out_arrival(turn, inner).wait_recv()
    out_ref[...] = out_block[...]
    for turn in range(1, SITES):
        for copy in query_copies(turn):
            copy.wait_send()
    for inner in range(site_heads):
        for turn in range(1, turns):
            kv_copy(turn, inner).wait_send()
        for turn in range(turns):
            pass_on(turn, inner).wait_send()
        for turn in range(1, SITES):
            out_copy(turn, inner).wait_send()


def gathered_body(query_rows, key_rows, value_rows, gate_logits, selection, cube_ids):
    token_count, feature_width = query_rows.shape
    head_count = gate_logits.shape[1] // 2
    head_size = feature_width // head_count
    local_cubes = token_count // CUBE
    total_cubes = cube_ids.shape[0]
    picks = selection.shape[2]
    cube_range = jnp.arange(total_cubes, dtype=jnp.int32)
    position = jnp.sum(
        jnp.where(cube_ids[None, :] == cube_range[:, None], cube_range[None, :], 0), axis=1
    )
    site_heads = head_count // SITES
    turns = SITES * HALVES
    block = (local_cubes, 2, CUBE, head_size)
    return pl.pallas_call(
        functools.partial(attention_kernel, (head_count, head_size, local_cubes, picks)),
        out_shape=jax.ShapeDtypeStruct((token_count, feature_width), jnp.bfloat16),
        in_specs=[pl.BlockSpec(memory_space=pltpu.SMEM)] * 2
        + [pl.BlockSpec(memory_space=pltpu.HBM)] * 4,
        out_specs=pl.BlockSpec(memory_space=pltpu.VMEM),
        scratch_shapes=[
            pltpu.VMEM((total_cubes, 2, CUBE, head_size), jnp.bfloat16)
            for unused in range(site_heads)
        ]
        + [
            pltpu.VMEM((SITES - 1, site_heads) + block, jnp.bfloat16),
            pltpu.VMEM((SITES, token_count, site_heads * head_size), jnp.bfloat16),
            pltpu.VMEM((SITES,) + gate_logits.shape, jnp.bfloat16),
            pltpu.VMEM((site_heads, SITES, token_count, head_size), jnp.bfloat16),
            pltpu.VMEM((token_count, feature_width), jnp.bfloat16),
            pltpu.SemaphoreType.DMA((site_heads, 2 * turns)),
            pltpu.SemaphoreType.DMA((site_heads, 2 * turns)),
            pltpu.SemaphoreType.DMA((2, SITES)),
            pltpu.SemaphoreType.DMA((2, SITES)),
            pltpu.SemaphoreType.DMA((site_heads, SITES)),
            pltpu.SemaphoreType.DMA((site_heads, SITES)),
            pltpu.SemaphoreType.DMA((SITES, site_heads, 2)),
            pltpu.SemaphoreType.DMA((2,)),
        ],
        compiler_params=pltpu.CompilerParams(
            collective_id=0, has_side_effects=True, vmem_limit_bytes=VMEM_GRANT
        ),
    )(
        position,
        selection.reshape(-1),
        query_rows,
        key_rows.reshape(local_cubes, CUBE, feature_width),
        value_rows.reshape(local_cubes, CUBE, feature_width),
        gate_logits,
    )


def body(query_rows, key_rows, value_rows, gate_logits, selection, cube_ids):
    device_count = lax.axis_size("cubes")
    head_count = gate_logits.shape[1] // 2
    fits = (
        device_count == CORES * SITES * HALVES
        and grid_of(device_count) == (2 * HALVES, SITES // 2)
        and head_count % SITES == 0
    )
    return (gathered_body if fits else streamed_body)(
        query_rows, key_rows, value_rows, gate_logits, selection, cube_ids
    )


def solution(mesh):
    placed = (
        P(("groups", "cubes"), None),
        P(("groups", "cubes"), None),
        P(("groups", "cubes"), None),
        P(("groups", "cubes"), None),
        P("groups", None, None),
        P("groups"),
    )
    return jax.shard_map(
        body, mesh=mesh, in_specs=placed, out_specs=P(("groups", "cubes"), None), check_vma=False
    )
```

```python
import functools
import math

import jax
import jax.numpy as jnp
from jax import lax
from jax.experimental import pallas as pl
from jax.experimental.pallas import tpu as pltpu
from jax.sharding import PartitionSpec as P

CUBE = 64
LOOKAHEAD = 3


NEG_START = -1e30


def block_partials(query_slots, pair_slots):
    head_size = query_slots.shape[-1]
    factor = 1.0 / math.sqrt(head_size)
    slot_keys = pair_slots[:, :, :head_size]
    slot_values = pair_slots[:, :, head_size:]
    scores = (
        jnp.einsum("sqd,skd->sqk", query_slots, slot_keys, preferred_element_type=jnp.float32)
        * factor
    )
    slot_max = jnp.max(scores, axis=2)
    weights = jnp.exp(scores - slot_max[:, :, None])
    slot_total = jnp.sum(weights, axis=2)
    numerator = jnp.einsum(
        "sqk,skd->sqd",
        weights.astype(jnp.bfloat16),
        slot_values,
        preferred_element_type=jnp.float32,
    )
    return (numerator, slot_max, slot_total)


def merge_slots(state, results, slot_group):
    numerator, running_max, totals = state
    slot_numerator, slot_max, slot_total = results
    group_count = numerator.shape[0]
    slot_count = slot_group.shape[0]
    member = slot_group[:, None] == jnp.arange(group_count, dtype=jnp.int32)[None, :]
    is_valid = slot_group >= 0
    group_max = jnp.max(jnp.where(member[:, :, None], slot_max[:, None, :], -jnp.inf), axis=0)
    new_max = jnp.maximum(running_max, group_max)
    slot_base = jnp.take(new_max, jnp.maximum(slot_group, 0), axis=0)
    slot_weight = jnp.exp(jnp.where(is_valid[:, None], slot_max - slot_base, -jnp.inf))
    onehot = member.astype(jnp.float32).T
    weighted = (slot_weight[:, :, None] * slot_numerator).reshape(slot_count, -1)
    added_numerator = jnp.dot(onehot, weighted, precision=lax.Precision.HIGHEST).reshape(
        numerator.shape
    )
    added_total = jnp.dot(onehot, slot_weight * slot_total, precision=lax.Precision.HIGHEST)
    decay_factor = jnp.exp(running_max - new_max)
    return (
        numerator * decay_factor[:, :, None] + added_numerator,
        new_max,
        totals * decay_factor + added_total,
    )


def streamed_body(query_rows, key_rows, value_rows, gate_logits, selection, cube_ids):
    device_count = lax.axis_size("cubes")
    token_count = query_rows.shape[0]
    feature_width = query_rows.shape[1]
    head_count = gate_logits.shape[1] // 2
    head_size = feature_width // head_count
    local_cubes = token_count // CUBE
    total_cubes = cube_ids.shape[0]
    picks_each = selection.shape[2]
    depth_rounds = max(2, head_count * picks_each // device_count + 1)
    request_count = local_cubes * head_count * picks_each
    factor = 1.0 / math.sqrt(head_size)
    self_index = lax.axis_index("cubes")
    pooled_keys = jnp.mean(
        key_rows.reshape(local_cubes, CUBE, feature_width), axis=1, dtype=jnp.float32
    ).astype(jnp.bfloat16)
    pooled_values = jnp.mean(
        value_rows.reshape(local_cubes, CUBE, feature_width), axis=1, dtype=jnp.float32
    ).astype(jnp.bfloat16)
    query_heads = query_rows.reshape(token_count, head_count, head_size)
    start_state = (
        jnp.zeros((head_count, token_count, head_size), jnp.float32),
        jnp.full((head_count, token_count), NEG_START, jnp.float32),
        jnp.zeros((head_count, token_count), jnp.float32),
    )
    numerator, running_max, totals = start_state
    piece_keys = lax.all_gather(pooled_keys, "cubes", axis=0, tiled=True)
    piece_values = lax.all_gather(pooled_values, "cubes", axis=0, tiled=True)
    piece_rows = piece_keys.shape[0]
    scores = (
        jnp.einsum(
            "thd,jhd->htj",
            query_heads,
            piece_keys.reshape(piece_rows, head_count, head_size),
            preferred_element_type=jnp.float32,
        )
        * factor
    )
    new_max = jnp.maximum(running_max, jnp.max(scores, axis=2))
    weights = jnp.exp(scores - new_max[:, :, None])
    added = jnp.einsum(
        "htj,jhd->htd",
        weights.astype(jnp.bfloat16),
        piece_values.reshape(piece_rows, head_count, head_size),
        preferred_element_type=jnp.float32,
    )
    numerator = added
    totals = jnp.sum(weights, axis=2)
    coarse = jnp.transpose(numerator / totals[:, :, None], (1, 0, 2))
    cube_range = jnp.arange(total_cubes, dtype=jnp.int32)
    position = jnp.sum(
        jnp.where(cube_ids[None, :] == cube_range[:, None], cube_range[None, :], 0), axis=1
    )
    targets = jnp.take(position, selection.reshape(-1)).reshape(device_count, request_count)
    request_range = jnp.arange(request_count, dtype=jnp.int32)
    request_group = request_range // picks_each
    request_head = request_group % head_count
    round_range = jnp.arange(depth_rounds, dtype=jnp.int32)
    own_targets = lax.dynamic_index_in_dim(targets, self_index, 0, keepdims=False)
    same_target = own_targets[:, None] == cube_range[None, :]
    running_count = jnp.cumsum(same_target.astype(jnp.int32), axis=0)
    own_rank = jnp.sum(jnp.where(same_target, running_count, 0), axis=1) - 1
    chosen_round = same_target[None, :, :] & (own_rank[None, :, None] == round_range[:, None, None])
    wanted_all = jnp.sum(jnp.where(chosen_round, request_group[None, :, None] + 1, 0), axis=1) - 1
    own_cubes = self_index * local_cubes + jnp.arange(local_cubes, dtype=jnp.int32)
    hit_mine = targets[:, :, None] == own_cubes[None, None, :]
    mine_rank = jnp.cumsum(hit_mine.astype(jnp.int32), axis=1) - 1
    round_hit = hit_mine[None] & (mine_rank[None] == round_range[:, None, None, None])
    incoming_all = (
        jnp.sum(jnp.where(round_hit, request_head[None, None, :, None] + 1, 0), axis=2) - 1
    )
    query_groups = (
        query_rows.reshape(local_cubes, CUBE, head_count, head_size)
        .transpose(0, 2, 1, 3)
        .reshape(local_cubes * head_count, CUBE, head_size)
    )
    pair_blocks = jnp.concatenate(
        (
            key_rows.reshape(local_cubes, CUBE, head_count, head_size),
            value_rows.reshape(local_cubes, CUBE, head_count, head_size),
        ),
        axis=3,
    )
    pair_groups = pair_blocks.transpose(0, 2, 1, 3).reshape(
        local_cubes * head_count, CUBE, 2 * head_size
    )
    base_group = head_count * jnp.arange(local_cubes, dtype=jnp.int32)

    def held_pairs(incoming):
        source = (jnp.maximum(incoming, 0) + base_group[None, :]).reshape(-1)
        picked = jnp.take(pair_groups, source, axis=0)
        return jnp.where(
            (incoming >= 0).reshape(-1)[:, None, None], picked, jnp.zeros((), jnp.bfloat16)
        )

    def asked_queries(wanted):
        picked = jnp.take(query_groups, jnp.maximum(wanted, 0), axis=0)
        return jnp.where((wanted >= 0)[:, None, None], picked, jnp.zeros((), jnp.bfloat16))

    def one_round(state, tables):
        wanted, incoming = tables
        arrived = lax.all_to_all(
            held_pairs(incoming), "cubes", split_axis=0, concat_axis=0, tiled=True
        )
        results = block_partials(asked_queries(wanted), arrived)
        return (merge_slots(state, results, wanted), None)

    group_count = local_cubes * head_count
    start_state = (
        jnp.zeros((group_count, CUBE, head_size), jnp.float32),
        jnp.full((group_count, CUBE), NEG_START, jnp.float32),
        jnp.zeros((group_count, CUBE), jnp.float32),
    )
    final_state, unused = lax.scan(one_round, start_state, (wanted_all, incoming_all))
    numerator, running_max, totals = final_state
    fine_groups = numerator / totals[:, :, None]
    fine = (
        fine_groups.reshape(local_cubes, head_count, CUBE, head_size)
        .transpose(0, 2, 1, 3)
        .reshape(token_count, head_count, head_size)
    )
    gates = jax.nn.sigmoid(gate_logits.astype(jnp.float32))
    mixed = gates[:, :head_count, None] * coarse + gates[:, head_count:, None] * fine
    return mixed.reshape(token_count, feature_width).astype(jnp.bfloat16)

CORES = 2
HALVES = 2
SITES = 4
VMEM_GRANT = 62 * 1024 * 1024


def grid_of(device_count):
    chips = device_count // CORES
    x_extent = 1
    for extent in range(1, chips + 1):
        if chips % extent == 0 and extent**3 <= chips:
            x_extent = extent
    return (chips // x_extent, x_extent)


def attention_kernel(
    sizes,
    cube_ids_ref,
    selection_ref,
    query_rows,
    key_cubes,
    value_cubes,
    gate_columns,
    out_ref,
    *scratch,
):
    head_count, head_size, local_cubes, picks = sizes
    site_heads = head_count // SITES
    buffers = scratch[:site_heads]
    (stage, query_ref, gate_turned, gate_ref, done, out_block, position_ref) = scratch[
        site_heads : site_heads + 7
    ]
    (kv_send, kv_recv, query_send, query_recv, out_send, out_recv, kv_local, query_local) = scratch[
        site_heads + 7 :
    ]
    factor = 1.0 / math.sqrt(head_size)
    width = site_heads * head_size
    me = lax.axis_index("cubes")
    core = me % CORES
    x = (me // CORES) % 2
    low = (me // (2 * CORES)) % 2
    half = me // (4 * CORES)
    sibling = me + 1 - 2 * core

    def flip(bit, on):
        return bit + on * (1 - 2 * bit)

    def device(turn):
        return (
            (flip(half, turn // 4) * 2 + flip(low, (turn // 2) % 2)) * 2 + flip(x, turn % 2)
        ) * CORES + core

    def group(turn):
        return flip(x, turn % 2) * 2 + flip(low, (turn // 2) % 2)

    def head_columns(head, count):
        return pl.ds(pl.multiple_of(head * head_size, head_size), count * head_size)

    def cubes_of(source):
        return pl.ds(source * local_cubes, local_cubes)

    def remote(source, target, send, recv, partner):
        return pltpu.make_async_remote_copy(
            src_ref=source,
            dst_ref=target,
            send_sem=send,
            recv_sem=recv,
            device_id={"cubes": partner},
            device_id_type=pl.DeviceIdType.MESH,
        )

    def held(turn, inner):
        if turn % SITES == 0:
            return buffers[inner].at[cubes_of(me)]
        return stage.at[turn % SITES - 1, inner]

    def fills(turn, inner):
        columns = head_columns(group(turn) * site_heads + inner, 1)
        return [
            pltpu.make_async_copy(
                ref.at[:, :, columns], held(turn, inner).at[:, kind], kv_local.at[turn, inner, kind]
            )
            for kind, ref in enumerate((key_cubes, value_cubes))
        ]

    def own_queries():
        columns = head_columns(group(0) * site_heads, site_heads)
        return [
            pltpu.make_async_copy(query_rows.at[:, columns], query_ref.at[0], query_local.at[0]),
            pltpu.make_async_copy(gate_columns, gate_turned, query_local.at[1]),
        ]

    def query_copies(turn):
        columns = head_columns(group(turn) * site_heads, site_heads)
        return [
            remote(
                query_rows.at[:, columns],
                query_ref.at[turn],
                query_send.at[0, turn],
                query_recv.at[0, turn],
                device(turn),
            ),
            remote(
                gate_ref.at[0],
                gate_ref.at[turn],
                query_send.at[1, turn],
                query_recv.at[1, turn],
                device(turn),
            ),
        ]

    def kv_copy(turn, inner):
        return remote(
            held(turn, inner),
            buffers[inner].at[cubes_of(me)],
            kv_send.at[inner, turn],
            kv_recv.at[inner, turn],
            device(turn),
        )

    def kv_arrival(turn, inner):
        region = buffers[inner].at[cubes_of(device(turn))]
        return remote(
            region, region, kv_send.at[inner, turn], kv_recv.at[inner, turn], device(turn)
        )

    turns = SITES * HALVES

    def pass_on(turn, inner):
        region = buffers[inner].at[cubes_of(device(turn))]
        slot = turns + turn
        return remote(region, region, kv_send.at[inner, slot], kv_recv.at[inner, slot], sibling)

    def passed_arrival(turn, inner):
        region = buffers[inner].at[cubes_of(device(turn) + 1 - 2 * core)]
        slot = turns + turn
        return remote(region, region, kv_send.at[inner, slot], kv_recv.at[inner, slot], sibling)

    def out_copy(turn, inner):
        columns = head_columns(group(0) * site_heads + inner, 1)
        return remote(
            done.at[inner, turn],
            out_block.at[:, columns],
            out_send.at[inner, turn],
            out_recv.at[inner, turn],
            device(turn),
        )

    def out_arrival(turn, inner):
        columns = head_columns(group(turn) * site_heads + inner, 1)
        return remote(
            done.at[inner, turn],
            out_block.at[:, columns],
            out_send.at[inner, turn],
            out_recv.at[inner, turn],
            device(turn),
        )

    def compute(inner):
        buffer = buffers[inner]
        head = group(0) * site_heads + inner
        columns = slice(inner * head_size, (inner + 1) * head_size)

        def pooled(kind):
            cubes = buffer[:, kind].astype(jnp.float32)
            return (jnp.sum(cubes, axis=1) * (1.0 / CUBE)).astype(jnp.bfloat16)

        pooled_keys = pooled(0)
        pooled_values = pooled(1)

        def softmax(queries, keys, values):
            scores = (
                lax.dot_general(
                    queries, keys, (((1,), (1,)), ((), ())), preferred_element_type=jnp.float32
                )
                * factor
            )
            weights = jnp.exp(scores - jnp.max(scores, axis=1, keepdims=True))
            total = jnp.sum(weights, axis=1, keepdims=True)
            return (
                jnp.dot(weights.astype(jnp.bfloat16), values, preferred_element_type=jnp.float32)
                / total
            )

        def one_turn(turn):
            queries = query_ref[turn, :, columns]
            coarse = softmax(queries, pooled_keys, pooled_values)
            gates = gate_ref[turn].astype(jnp.float32)
            lane = lax.broadcasted_iota(jnp.int32, gates.shape, 1)
            coarse_gate = jax.nn.sigmoid(
                jnp.sum(jnp.where(lane == head, gates, 0.0), axis=1, keepdims=True)
            )
            fine_gate = jax.nn.sigmoid(
                jnp.sum(jnp.where(lane == head + head_count, gates, 0.0), axis=1, keepdims=True)
            )
            fine = []
            for cube in range(local_cubes):
                block = device(turn) * local_cubes + cube
                chosen = [position_ref[selection_ref[head, pick, block]] for pick in range(picks)]
                keys = jnp.concatenate([buffer[t, 0] for t in chosen], axis=0)
                values = jnp.concatenate([buffer[t, 1] for t in chosen], axis=0)
                fine.append(softmax(queries[cube * CUBE : (cube + 1) * CUBE], keys, values))
            fine = jnp.concatenate(fine, axis=0)
            return (coarse_gate * coarse + fine_gate * fine).astype(done.dtype)

        for pair in ((3, 2), (1, 0)):
            results = [one_turn(turn) for turn in pair]
            for turn, result in zip(pair, results):
                if turn == 0:
                    out_block[:, head_columns(head, 1)] = result
                else:
                    done[inner, turn] = result
            for turn in pair:
                if turn != 0:
                    out_copy(turn, inner).start()

    far_first = (7, 6, 5, 4, 3, 2, 1)

    def send(inner):
        for turn in range(SITES):
            for copy in fills(turn, inner):
                copy.wait()
        for turn in far_first:
            kv_copy(turn, inner).start()
        pass_on(0, inner).start()

    for copy in own_queries():
        copy.start()
    for inner in range(site_heads):
        for turn in range(SITES):
            for copy in fills(turn, inner):
                copy.start()
    barrier = pltpu.get_barrier_semaphore()
    for partner in [sibling] + [device(turn) for turn in range(1, turns)]:
        pl.semaphore_signal(
            barrier, inc=1, device_id={"cubes": partner}, device_id_type=pl.DeviceIdType.MESH
        )
    pl.semaphore_wait(barrier, turns)
    for copy in own_queries():
        copy.wait()
    gate_ref[0] = gate_turned[...].astype(jnp.float32).T.astype(gate_ref.dtype)
    for turn in range(1, SITES):
        for copy in query_copies(turn):
            copy.start()
    for inner in range(min(LOOKAHEAD, site_heads)):
        send(inner)

    def place(cube, carry):
        found = jnp.int32(0)
        for block in range(cube_ids_ref.shape[0]):
            found = jnp.where(cube_ids_ref[block] == cube, block, found)
        position_ref[cube] = found
        return carry

    lax.fori_loop(0, cube_ids_ref.shape[0], place, 0)
    for inner in range(site_heads):
        for turn in range(1, turns):
            kv_arrival(turn, inner).wait_recv()
            pass_on(turn, inner).start()
        if inner + LOOKAHEAD < site_heads:
            send(inner + LOOKAHEAD)
        if inner == 0:
            for turn in range(1, SITES):
                for copy in query_copies(turn):
                    copy.wait_recv()
        for turn in range(turns):
            passed_arrival(turn, inner).wait_recv()
        compute(inner)
    for inner in range(site_heads):
        for turn in range(1, SITES):
            out_arrival(turn, inner).wait_recv()
    out_ref[...] = out_block[...]
    for turn in range(1, SITES):
        for copy in query_copies(turn):
            copy.wait_send()
    for inner in range(site_heads):
        for turn in range(1, turns):
            kv_copy(turn, inner).wait_send()
        for turn in range(turns):
            pass_on(turn, inner).wait_send()
        for turn in range(1, SITES):
            out_copy(turn, inner).wait_send()


def gathered_body(query_rows, key_rows, value_rows, gate_logits, selection, cube_ids):
    token_count, feature_width = query_rows.shape
    head_count = gate_logits.shape[1] // 2
    head_size = feature_width // head_count
    local_cubes = token_count // CUBE
    total_cubes = cube_ids.shape[0]
    picks = selection.shape[2]
    site_heads = head_count // SITES
    turns = SITES * HALVES
    block = (local_cubes, 2, CUBE, head_size)
    return pl.pallas_call(
        functools.partial(attention_kernel, (head_count, head_size, local_cubes, picks)),
        out_shape=jax.ShapeDtypeStruct((token_count, feature_width), jnp.bfloat16),
        in_specs=[pl.BlockSpec(memory_space=pltpu.SMEM)] * 2
        + [pl.BlockSpec(memory_space=pltpu.HBM)] * 4,
        out_specs=pl.BlockSpec(memory_space=pltpu.VMEM),
        scratch_shapes=[
            pltpu.VMEM((total_cubes, 2, CUBE, head_size), jnp.bfloat16)
            for unused in range(site_heads)
        ]
        + [
            pltpu.VMEM((SITES - 1, site_heads) + block, jnp.bfloat16),
            pltpu.VMEM((SITES, token_count, site_heads * head_size), jnp.bfloat16),
            pltpu.VMEM(gate_logits.shape[::-1], jnp.bfloat16),
            pltpu.VMEM((SITES,) + gate_logits.shape, jnp.bfloat16),
            pltpu.VMEM((site_heads, SITES, token_count, head_size), jnp.bfloat16),
            pltpu.VMEM((token_count, feature_width), jnp.bfloat16),
            pltpu.SMEM((total_cubes,), jnp.int32),
            pltpu.SemaphoreType.DMA((site_heads, 2 * turns)),
            pltpu.SemaphoreType.DMA((site_heads, 2 * turns)),
            pltpu.SemaphoreType.DMA((2, SITES)),
            pltpu.SemaphoreType.DMA((2, SITES)),
            pltpu.SemaphoreType.DMA((site_heads, SITES)),
            pltpu.SemaphoreType.DMA((site_heads, SITES)),
            pltpu.SemaphoreType.DMA((SITES, site_heads, 2)),
            pltpu.SemaphoreType.DMA((2,)),
        ],
        compiler_params=pltpu.CompilerParams(
            collective_id=0, has_side_effects=True, vmem_limit_bytes=VMEM_GRANT
        ),
    )(
        cube_ids,
        selection.transpose(1, 2, 0),
        query_rows,
        key_rows.reshape(local_cubes, CUBE, feature_width),
        value_rows.reshape(local_cubes, CUBE, feature_width),
        gate_logits.T,
    )


def body(query_rows, key_rows, value_rows, gate_logits, selection, cube_ids):
    device_count = lax.axis_size("cubes")
    head_count = gate_logits.shape[1] // 2
    fits = (
        device_count == CORES * SITES * HALVES
        and grid_of(device_count) == (2 * HALVES, SITES // 2)
        and head_count % SITES == 0
    )
    return (gathered_body if fits else streamed_body)(
        query_rows, key_rows, value_rows, gate_logits, selection, cube_ids
    )


def solution(mesh):
    placed = (
        P(("groups", "cubes"), None),
        P(("groups", "cubes"), None),
        P(("groups", "cubes"), None),
        P(("groups", "cubes"), None),
        P("groups", None, None),
        P("groups"),
    )
    return jax.shard_map(
        body, mesh=mesh, in_specs=placed, out_specs=P(("groups", "cubes"), None), check_vma=False
    )
```

```python
import functools
import math

import jax
import jax.numpy as jnp
from jax import lax
from jax.experimental import pallas as pl
from jax.experimental.pallas import tpu as pltpu
from jax.sharding import PartitionSpec as P

CUBE = 64
LOOKAHEAD = 2


NEG_START = -1e30


def block_partials(query_slots, pair_slots):
    head_size = query_slots.shape[-1]
    factor = 1.0 / math.sqrt(head_size)
    slot_keys = pair_slots[:, :, :head_size]
    slot_values = pair_slots[:, :, head_size:]
    scores = (
        jnp.einsum("sqd,skd->sqk", query_slots, slot_keys, preferred_element_type=jnp.float32)
        * factor
    )
    slot_max = jnp.max(scores, axis=2)
    weights = jnp.exp(scores - slot_max[:, :, None])
    slot_total = jnp.sum(weights, axis=2)
    numerator = jnp.einsum(
        "sqk,skd->sqd",
        weights.astype(jnp.bfloat16),
        slot_values,
        preferred_element_type=jnp.float32,
    )
    return (numerator, slot_max, slot_total)


def merge_slots(state, results, slot_group):
    numerator, running_max, totals = state
    slot_numerator, slot_max, slot_total = results
    group_count = numerator.shape[0]
    slot_count = slot_group.shape[0]
    member = slot_group[:, None] == jnp.arange(group_count, dtype=jnp.int32)[None, :]
    is_valid = slot_group >= 0
    group_max = jnp.max(jnp.where(member[:, :, None], slot_max[:, None, :], -jnp.inf), axis=0)
    new_max = jnp.maximum(running_max, group_max)
    slot_base = jnp.take(new_max, jnp.maximum(slot_group, 0), axis=0)
    slot_weight = jnp.exp(jnp.where(is_valid[:, None], slot_max - slot_base, -jnp.inf))
    onehot = member.astype(jnp.float32).T
    weighted = (slot_weight[:, :, None] * slot_numerator).reshape(slot_count, -1)
    added_numerator = jnp.dot(onehot, weighted, precision=lax.Precision.HIGHEST).reshape(
        numerator.shape
    )
    added_total = jnp.dot(onehot, slot_weight * slot_total, precision=lax.Precision.HIGHEST)
    decay_factor = jnp.exp(running_max - new_max)
    return (
        numerator * decay_factor[:, :, None] + added_numerator,
        new_max,
        totals * decay_factor + added_total,
    )


def streamed_body(query_rows, key_rows, value_rows, gate_logits, selection, cube_ids):
    device_count = lax.axis_size("cubes")
    token_count = query_rows.shape[0]
    feature_width = query_rows.shape[1]
    head_count = gate_logits.shape[1] // 2
    head_size = feature_width // head_count
    local_cubes = token_count // CUBE
    total_cubes = cube_ids.shape[0]
    picks_each = selection.shape[2]
    depth_rounds = max(2, head_count * picks_each // device_count + 1)
    request_count = local_cubes * head_count * picks_each
    factor = 1.0 / math.sqrt(head_size)
    self_index = lax.axis_index("cubes")
    pooled_keys = jnp.mean(
        key_rows.reshape(local_cubes, CUBE, feature_width), axis=1, dtype=jnp.float32
    ).astype(jnp.bfloat16)
    pooled_values = jnp.mean(
        value_rows.reshape(local_cubes, CUBE, feature_width), axis=1, dtype=jnp.float32
    ).astype(jnp.bfloat16)
    query_heads = query_rows.reshape(token_count, head_count, head_size)
    start_state = (
        jnp.zeros((head_count, token_count, head_size), jnp.float32),
        jnp.full((head_count, token_count), NEG_START, jnp.float32),
        jnp.zeros((head_count, token_count), jnp.float32),
    )
    numerator, running_max, totals = start_state
    piece_keys = lax.all_gather(pooled_keys, "cubes", axis=0, tiled=True)
    piece_values = lax.all_gather(pooled_values, "cubes", axis=0, tiled=True)
    piece_rows = piece_keys.shape[0]
    scores = (
        jnp.einsum(
            "thd,jhd->htj",
            query_heads,
            piece_keys.reshape(piece_rows, head_count, head_size),
            preferred_element_type=jnp.float32,
        )
        * factor
    )
    new_max = jnp.maximum(running_max, jnp.max(scores, axis=2))
    weights = jnp.exp(scores - new_max[:, :, None])
    added = jnp.einsum(
        "htj,jhd->htd",
        weights.astype(jnp.bfloat16),
        piece_values.reshape(piece_rows, head_count, head_size),
        preferred_element_type=jnp.float32,
    )
    numerator = added
    totals = jnp.sum(weights, axis=2)
    coarse = jnp.transpose(numerator / totals[:, :, None], (1, 0, 2))
    cube_range = jnp.arange(total_cubes, dtype=jnp.int32)
    position = jnp.sum(
        jnp.where(cube_ids[None, :] == cube_range[:, None], cube_range[None, :], 0), axis=1
    )
    targets = jnp.take(position, selection.reshape(-1)).reshape(device_count, request_count)
    request_range = jnp.arange(request_count, dtype=jnp.int32)
    request_group = request_range // picks_each
    request_head = request_group % head_count
    round_range = jnp.arange(depth_rounds, dtype=jnp.int32)
    own_targets = lax.dynamic_index_in_dim(targets, self_index, 0, keepdims=False)
    same_target = own_targets[:, None] == cube_range[None, :]
    running_count = jnp.cumsum(same_target.astype(jnp.int32), axis=0)
    own_rank = jnp.sum(jnp.where(same_target, running_count, 0), axis=1) - 1
    chosen_round = same_target[None, :, :] & (own_rank[None, :, None] == round_range[:, None, None])
    wanted_all = jnp.sum(jnp.where(chosen_round, request_group[None, :, None] + 1, 0), axis=1) - 1
    own_cubes = self_index * local_cubes + jnp.arange(local_cubes, dtype=jnp.int32)
    hit_mine = targets[:, :, None] == own_cubes[None, None, :]
    mine_rank = jnp.cumsum(hit_mine.astype(jnp.int32), axis=1) - 1
    round_hit = hit_mine[None] & (mine_rank[None] == round_range[:, None, None, None])
    incoming_all = (
        jnp.sum(jnp.where(round_hit, request_head[None, None, :, None] + 1, 0), axis=2) - 1
    )
    query_groups = (
        query_rows.reshape(local_cubes, CUBE, head_count, head_size)
        .transpose(0, 2, 1, 3)
        .reshape(local_cubes * head_count, CUBE, head_size)
    )
    pair_blocks = jnp.concatenate(
        (
            key_rows.reshape(local_cubes, CUBE, head_count, head_size),
            value_rows.reshape(local_cubes, CUBE, head_count, head_size),
        ),
        axis=3,
    )
    pair_groups = pair_blocks.transpose(0, 2, 1, 3).reshape(
        local_cubes * head_count, CUBE, 2 * head_size
    )
    base_group = head_count * jnp.arange(local_cubes, dtype=jnp.int32)

    def held_pairs(incoming):
        source = (jnp.maximum(incoming, 0) + base_group[None, :]).reshape(-1)
        picked = jnp.take(pair_groups, source, axis=0)
        return jnp.where(
            (incoming >= 0).reshape(-1)[:, None, None], picked, jnp.zeros((), jnp.bfloat16)
        )

    def asked_queries(wanted):
        picked = jnp.take(query_groups, jnp.maximum(wanted, 0), axis=0)
        return jnp.where((wanted >= 0)[:, None, None], picked, jnp.zeros((), jnp.bfloat16))

    def one_round(state, tables):
        wanted, incoming = tables
        arrived = lax.all_to_all(
            held_pairs(incoming), "cubes", split_axis=0, concat_axis=0, tiled=True
        )
        results = block_partials(asked_queries(wanted), arrived)
        return (merge_slots(state, results, wanted), None)

    group_count = local_cubes * head_count
    start_state = (
        jnp.zeros((group_count, CUBE, head_size), jnp.float32),
        jnp.full((group_count, CUBE), NEG_START, jnp.float32),
        jnp.zeros((group_count, CUBE), jnp.float32),
    )
    final_state, unused = lax.scan(one_round, start_state, (wanted_all, incoming_all))
    numerator, running_max, totals = final_state
    fine_groups = numerator / totals[:, :, None]
    fine = (
        fine_groups.reshape(local_cubes, head_count, CUBE, head_size)
        .transpose(0, 2, 1, 3)
        .reshape(token_count, head_count, head_size)
    )
    gates = jax.nn.sigmoid(gate_logits.astype(jnp.float32))
    mixed = gates[:, :head_count, None] * coarse + gates[:, head_count:, None] * fine
    return mixed.reshape(token_count, feature_width).astype(jnp.bfloat16)

CORES = 2
HALVES = 2
SITES = 4
VMEM_GRANT = 62 * 1024 * 1024


def grid_of(device_count):
    chips = device_count // CORES
    x_extent = 1
    for extent in range(1, chips + 1):
        if chips % extent == 0 and extent**3 <= chips:
            x_extent = extent
    return (chips // x_extent, x_extent)


def attention_kernel(
    sizes,
    cube_ids_ref,
    selection_ref,
    query_rows,
    key_cubes,
    value_cubes,
    gate_columns,
    out_ref,
    *scratch,
):
    head_count, head_size, local_cubes, picks = sizes
    site_heads = head_count // SITES
    buffers = scratch[:site_heads]
    (stage, query_ref, gate_turned, gate_ref, done, out_block, position_ref) = scratch[
        site_heads : site_heads + 7
    ]
    (kv_send, kv_recv, query_send, query_recv, out_send, out_recv, kv_local, query_local) = scratch[
        site_heads + 7 :
    ]
    factor = math.log2(math.e) / math.sqrt(head_size)
    me = lax.axis_index("cubes")
    core = me % CORES
    x = (me // CORES) % 2
    low = (me // (2 * CORES)) % 2
    half = me // (4 * CORES)
    sibling = me + 1 - 2 * core

    def flip(bit, on):
        return bit + on * (1 - 2 * bit)

    def device(turn):
        return (
            (flip(half, turn // 4) * 2 + flip(low, (turn // 2) % 2)) * 2 + flip(x, turn % 2)
        ) * CORES + core

    def group(turn):
        return flip(x, turn % 2) * 2 + flip(low, (turn // 2) % 2)

    def head_columns(head, count):
        return pl.ds(pl.multiple_of(head * head_size, head_size), count * head_size)

    def cubes_of(source):
        return pl.ds(source * local_cubes, local_cubes)

    def remote(source, target, send, recv, partner):
        return pltpu.make_async_remote_copy(
            src_ref=source,
            dst_ref=target,
            send_sem=send,
            recv_sem=recv,
            device_id={"cubes": partner},
            device_id_type=pl.DeviceIdType.MESH,
        )

    def held(turn, inner):
        if turn % SITES == 0:
            return buffers[inner].at[cubes_of(me)]
        return stage.at[turn % SITES - 1, inner]

    def fills(turn, inner):
        columns = head_columns(group(turn) * site_heads + inner, 1)
        return [
            pltpu.make_async_copy(
                ref.at[:, :, columns], held(turn, inner).at[:, kind], kv_local.at[turn, inner, kind]
            )
            for kind, ref in enumerate((key_cubes, value_cubes))
        ]

    def own_queries():
        columns = head_columns(group(0) * site_heads, site_heads)
        return [
            pltpu.make_async_copy(query_rows.at[:, columns], query_ref.at[0], query_local.at[0]),
            pltpu.make_async_copy(gate_columns, gate_turned, query_local.at[1]),
        ]

    def query_copies(turn):
        columns = head_columns(group(turn) * site_heads, site_heads)
        return [
            remote(
                query_rows.at[:, columns],
                query_ref.at[turn],
                query_send.at[0, turn],
                query_recv.at[0, turn],
                device(turn),
            ),
            remote(
                gate_ref.at[0],
                gate_ref.at[turn],
                query_send.at[1, turn],
                query_recv.at[1, turn],
                device(turn),
            ),
        ]

    def kv_copy(turn, inner):
        return remote(
            held(turn, inner),
            buffers[inner].at[cubes_of(me)],
            kv_send.at[inner, turn],
            kv_recv.at[inner, turn],
            device(turn),
        )

    def kv_arrival(turn, inner):
        region = buffers[inner].at[cubes_of(device(turn))]
        return remote(
            region, region, kv_send.at[inner, turn], kv_recv.at[inner, turn], device(turn)
        )

    turns = SITES * HALVES

    def pass_on(turn, inner):
        region = buffers[inner].at[cubes_of(device(turn))]
        slot = turns + turn
        return remote(region, region, kv_send.at[inner, slot], kv_recv.at[inner, slot], sibling)

    def passed_arrival(turn, inner):
        region = buffers[inner].at[cubes_of(device(turn) + 1 - 2 * core)]
        slot = turns + turn
        return remote(region, region, kv_send.at[inner, slot], kv_recv.at[inner, slot], sibling)

    def out_copy(turn, inner):
        return remote(
            done.at[inner, turn],
            out_block.at[:, head_columns(group(0) * site_heads + inner, 1)],
            out_send.at[inner, turn],
            out_recv.at[inner, turn],
            device(turn),
        )

    def out_arrival(turn, inner):
        return remote(
            done.at[inner, turn],
            out_block.at[:, head_columns(group(turn) * site_heads + inner, 1)],
            out_send.at[inner, turn],
            out_recv.at[inner, turn],
            device(turn),
        )

    def compute(inner):
        buffer = buffers[inner]
        head = group(0) * site_heads + inner
        columns = slice(inner * head_size, (inner + 1) * head_size)

        def pooled(kind):
            cubes = buffer[:, kind].astype(jnp.float32)
            return (jnp.sum(cubes, axis=1) * (1.0 / CUBE)).astype(jnp.bfloat16)

        pooled_keys = pooled(0)
        pooled_values = pooled(1)

        def softmax(queries, keys, values):
            scores = lax.dot_general(
                queries, keys, (((1,), (1,)), ((), ())), preferred_element_type=jnp.float32
            )
            weights = jnp.exp2((scores - jnp.max(scores, axis=1, keepdims=True)) * factor)
            total = jnp.sum(weights, axis=1, keepdims=True)
            return (
                jnp.dot(weights.astype(jnp.bfloat16), values, preferred_element_type=jnp.float32)
                / total
            )

        def one_turn(turn):
            queries = query_ref[turn, :, columns]
            coarse = softmax(queries, pooled_keys, pooled_values)
            gates = gate_ref[turn].astype(jnp.float32)
            lane = lax.broadcasted_iota(jnp.int32, gates.shape, 1)
            coarse_gate = jax.nn.sigmoid(
                jnp.sum(jnp.where(lane == head, gates, 0.0), axis=1, keepdims=True)
            )
            fine_gate = jax.nn.sigmoid(
                jnp.sum(jnp.where(lane == head + head_count, gates, 0.0), axis=1, keepdims=True)
            )
            fine = []
            for cube in range(local_cubes):
                block = device(turn) * local_cubes + cube
                chosen = [position_ref[selection_ref[head, pick, block]] for pick in range(picks)]
                keys = jnp.concatenate([buffer[t, 0] for t in chosen], axis=0)
                values = jnp.concatenate([buffer[t, 1] for t in chosen], axis=0)
                fine.append(softmax(queries[cube * CUBE : (cube + 1) * CUBE], keys, values))
            fine = jnp.concatenate(fine, axis=0)
            return (coarse_gate * coarse + fine_gate * fine).astype(done.dtype)

        for pair in ((3, 2), (1, 0)):
            results = [one_turn(turn) for turn in pair]
            for turn, result in zip(pair, results):
                if turn == 0:
                    out_block[:, head_columns(head, 1)] = result
                else:
                    done[inner, turn] = result
            for turn in pair:
                if turn != 0:
                    out_copy(turn, inner).start()

    far_first = (7, 6, 5, 4, 3, 2, 1)

    def send(inner):
        for turn in range(SITES):
            for copy in fills(turn, inner):
                copy.wait()
        for turn in far_first:
            kv_copy(turn, inner).start()
        pass_on(0, inner).start()

    for copy in own_queries():
        copy.start()
    for inner in range(site_heads):
        for turn in range(SITES):
            for copy in fills(turn, inner):
                copy.start()
    barrier = pltpu.get_barrier_semaphore()
    for partner in [sibling] + [device(turn) for turn in range(1, turns)]:
        pl.semaphore_signal(
            barrier, inc=1, device_id={"cubes": partner}, device_id_type=pl.DeviceIdType.MESH
        )
    pl.semaphore_wait(barrier, turns)
    for copy in own_queries():
        copy.wait()
    gate_ref[0] = gate_turned[...].astype(jnp.float32).T.astype(gate_ref.dtype)
    for turn in range(1, SITES):
        for copy in query_copies(turn):
            copy.start()
    for inner in range(min(LOOKAHEAD, site_heads)):
        send(inner)

    def place(cube, carry):
        found = jnp.int32(0)
        for block in range(cube_ids_ref.shape[0]):
            found = jnp.where(cube_ids_ref[block] == cube, block, found)
        position_ref[cube] = found
        return carry

    lax.fori_loop(0, cube_ids_ref.shape[0], place, 0)
    for inner in range(min(LOOKAHEAD, site_heads), site_heads):
        for turn in range(SITES):
            for copy in fills(turn, inner):
                copy.wait()
    for inner in range(site_heads):
        for turn in range(1, turns):
            kv_arrival(turn, inner).wait_recv()
            pass_on(turn, inner).start()
            if inner + LOOKAHEAD < site_heads:
                kv_copy(turn, inner + LOOKAHEAD).start()
        if inner + LOOKAHEAD < site_heads:
            pass_on(0, inner + LOOKAHEAD).start()
        if inner == 0:
            for turn in range(1, SITES):
                for copy in query_copies(turn):
                    copy.wait_recv()
        for turn in range(turns):
            passed_arrival(turn, inner).wait_recv()
        compute(inner)
    for inner in range(site_heads):
        for turn in range(1, SITES):
            out_arrival(turn, inner).wait_recv()
    out_ref[...] = out_block[...].astype(out_ref.dtype)
    for turn in range(1, SITES):
        for copy in query_copies(turn):
            copy.wait_send()
    for inner in range(site_heads):
        for turn in range(1, turns):
            kv_copy(turn, inner).wait_send()
        for turn in range(turns):
            pass_on(turn, inner).wait_send()
        for turn in range(1, SITES):
            out_copy(turn, inner).wait_send()


def gathered_body(query_rows, key_rows, value_rows, gate_logits, selection, cube_ids):
    token_count, feature_width = query_rows.shape
    head_count = gate_logits.shape[1] // 2
    head_size = feature_width // head_count
    local_cubes = token_count // CUBE
    total_cubes = cube_ids.shape[0]
    picks = selection.shape[2]
    site_heads = head_count // SITES
    turns = SITES * HALVES
    block = (local_cubes, 2, CUBE, head_size)
    mixed = pl.pallas_call(
        functools.partial(attention_kernel, (head_count, head_size, local_cubes, picks)),
        out_shape=jax.ShapeDtypeStruct((token_count, feature_width), jnp.float32),
        in_specs=[pl.BlockSpec(memory_space=pltpu.SMEM)] * 2
        + [pl.BlockSpec(memory_space=pltpu.HBM)] * 4,
        out_specs=pl.BlockSpec(memory_space=pltpu.VMEM),
        scratch_shapes=[
            pltpu.VMEM((total_cubes, 2, CUBE, head_size), jnp.bfloat16)
            for unused in range(site_heads)
        ]
        + [
            pltpu.VMEM((SITES - 1, site_heads) + block, jnp.bfloat16),
            pltpu.VMEM((SITES, token_count, site_heads * head_size), jnp.bfloat16),
            pltpu.VMEM(gate_logits.shape[::-1], jnp.bfloat16),
            pltpu.VMEM((SITES,) + gate_logits.shape, jnp.bfloat16),
            pltpu.VMEM((site_heads, SITES, token_count, head_size), jnp.bfloat16),
            pltpu.VMEM((token_count, feature_width), jnp.bfloat16),
            pltpu.SMEM((total_cubes,), jnp.int32),
            pltpu.SemaphoreType.DMA((site_heads, 2 * turns)),
            pltpu.SemaphoreType.DMA((site_heads, 2 * turns)),
            pltpu.SemaphoreType.DMA((2, SITES)),
            pltpu.SemaphoreType.DMA((2, SITES)),
            pltpu.SemaphoreType.DMA((site_heads, SITES)),
            pltpu.SemaphoreType.DMA((site_heads, SITES)),
            pltpu.SemaphoreType.DMA((SITES, site_heads, 2)),
            pltpu.SemaphoreType.DMA((2,)),
        ],
        compiler_params=pltpu.CompilerParams(
            collective_id=0, has_side_effects=True, vmem_limit_bytes=VMEM_GRANT
        ),
    )(
        cube_ids,
        selection.transpose(1, 2, 0),
        query_rows,
        key_rows.reshape(local_cubes, CUBE, feature_width),
        value_rows.reshape(local_cubes, CUBE, feature_width),
        gate_logits.T,
    )
    return mixed.astype(jnp.bfloat16)


def body(query_rows, key_rows, value_rows, gate_logits, selection, cube_ids):
    device_count = lax.axis_size("cubes")
    head_count = gate_logits.shape[1] // 2
    fits = (
        device_count == CORES * SITES * HALVES
        and grid_of(device_count) == (2 * HALVES, SITES // 2)
        and head_count % SITES == 0
    )
    return (gathered_body if fits else streamed_body)(
        query_rows, key_rows, value_rows, gate_logits, selection, cube_ids
    )


def solution(mesh):
    placed = (
        P(("groups", "cubes"), None),
        P(("groups", "cubes"), None),
        P(("groups", "cubes"), None),
        P(("groups", "cubes"), None),
        P("groups", None, None),
        P("groups"),
    )
    return jax.shard_map(
        body, mesh=mesh, in_specs=placed, out_specs=P(("groups", "cubes"), None), check_vma=False
    )
```

```python
import functools
import math

import jax
import jax.numpy as jnp
from jax import lax
from jax.experimental import pallas as pl
from jax.experimental.pallas import tpu as pltpu
from jax.sharding import PartitionSpec as P

CUBE = 64
LOOKAHEAD = 5


NEG_START = -1e30


def block_partials(query_slots, pair_slots):
    head_size = query_slots.shape[-1]
    factor = 1.0 / math.sqrt(head_size)
    slot_keys = pair_slots[:, :, :head_size]
    slot_values = pair_slots[:, :, head_size:]
    scores = (
        jnp.einsum("sqd,skd->sqk", query_slots, slot_keys, preferred_element_type=jnp.float32)
        * factor
    )
    slot_max = jnp.max(scores, axis=2)
    weights = jnp.exp(scores - slot_max[:, :, None])
    slot_total = jnp.sum(weights, axis=2)
    numerator = jnp.einsum(
        "sqk,skd->sqd",
        weights.astype(jnp.bfloat16),
        slot_values,
        preferred_element_type=jnp.float32,
    )
    return (numerator, slot_max, slot_total)


def merge_slots(state, results, slot_group):
    numerator, running_max, totals = state
    slot_numerator, slot_max, slot_total = results
    group_count = numerator.shape[0]
    slot_count = slot_group.shape[0]
    member = slot_group[:, None] == jnp.arange(group_count, dtype=jnp.int32)[None, :]
    is_valid = slot_group >= 0
    group_max = jnp.max(jnp.where(member[:, :, None], slot_max[:, None, :], -jnp.inf), axis=0)
    new_max = jnp.maximum(running_max, group_max)
    slot_base = jnp.take(new_max, jnp.maximum(slot_group, 0), axis=0)
    slot_weight = jnp.exp(jnp.where(is_valid[:, None], slot_max - slot_base, -jnp.inf))
    onehot = member.astype(jnp.float32).T
    weighted = (slot_weight[:, :, None] * slot_numerator).reshape(slot_count, -1)
    added_numerator = jnp.dot(onehot, weighted, precision=lax.Precision.HIGHEST).reshape(
        numerator.shape
    )
    added_total = jnp.dot(onehot, slot_weight * slot_total, precision=lax.Precision.HIGHEST)
    decay_factor = jnp.exp(running_max - new_max)
    return (
        numerator * decay_factor[:, :, None] + added_numerator,
        new_max,
        totals * decay_factor + added_total,
    )


def streamed_body(query_rows, key_rows, value_rows, gate_logits, selection, cube_ids):
    device_count = lax.axis_size("cubes")
    token_count = query_rows.shape[0]
    feature_width = query_rows.shape[1]
    head_count = gate_logits.shape[1] // 2
    head_size = feature_width // head_count
    local_cubes = token_count // CUBE
    total_cubes = cube_ids.shape[0]
    picks_each = selection.shape[2]
    depth_rounds = max(2, head_count * picks_each // device_count + 1)
    request_count = local_cubes * head_count * picks_each
    factor = 1.0 / math.sqrt(head_size)
    self_index = lax.axis_index("cubes")
    pooled_keys = jnp.mean(
        key_rows.reshape(local_cubes, CUBE, feature_width), axis=1, dtype=jnp.float32
    ).astype(jnp.bfloat16)
    pooled_values = jnp.mean(
        value_rows.reshape(local_cubes, CUBE, feature_width), axis=1, dtype=jnp.float32
    ).astype(jnp.bfloat16)
    query_heads = query_rows.reshape(token_count, head_count, head_size)
    start_state = (
        jnp.zeros((head_count, token_count, head_size), jnp.float32),
        jnp.full((head_count, token_count), NEG_START, jnp.float32),
        jnp.zeros((head_count, token_count), jnp.float32),
    )
    numerator, running_max, totals = start_state
    piece_keys = lax.all_gather(pooled_keys, "cubes", axis=0, tiled=True)
    piece_values = lax.all_gather(pooled_values, "cubes", axis=0, tiled=True)
    piece_rows = piece_keys.shape[0]
    scores = (
        jnp.einsum(
            "thd,jhd->htj",
            query_heads,
            piece_keys.reshape(piece_rows, head_count, head_size),
            preferred_element_type=jnp.float32,
        )
        * factor
    )
    new_max = jnp.maximum(running_max, jnp.max(scores, axis=2))
    weights = jnp.exp(scores - new_max[:, :, None])
    added = jnp.einsum(
        "htj,jhd->htd",
        weights.astype(jnp.bfloat16),
        piece_values.reshape(piece_rows, head_count, head_size),
        preferred_element_type=jnp.float32,
    )
    numerator = added
    totals = jnp.sum(weights, axis=2)
    coarse = jnp.transpose(numerator / totals[:, :, None], (1, 0, 2))
    cube_range = jnp.arange(total_cubes, dtype=jnp.int32)
    position = jnp.sum(
        jnp.where(cube_ids[None, :] == cube_range[:, None], cube_range[None, :], 0), axis=1
    )
    targets = jnp.take(position, selection.reshape(-1)).reshape(device_count, request_count)
    request_range = jnp.arange(request_count, dtype=jnp.int32)
    request_group = request_range // picks_each
    request_head = request_group % head_count
    round_range = jnp.arange(depth_rounds, dtype=jnp.int32)
    own_targets = lax.dynamic_index_in_dim(targets, self_index, 0, keepdims=False)
    same_target = own_targets[:, None] == cube_range[None, :]
    running_count = jnp.cumsum(same_target.astype(jnp.int32), axis=0)
    own_rank = jnp.sum(jnp.where(same_target, running_count, 0), axis=1) - 1
    chosen_round = same_target[None, :, :] & (own_rank[None, :, None] == round_range[:, None, None])
    wanted_all = jnp.sum(jnp.where(chosen_round, request_group[None, :, None] + 1, 0), axis=1) - 1
    own_cubes = self_index * local_cubes + jnp.arange(local_cubes, dtype=jnp.int32)
    hit_mine = targets[:, :, None] == own_cubes[None, None, :]
    mine_rank = jnp.cumsum(hit_mine.astype(jnp.int32), axis=1) - 1
    round_hit = hit_mine[None] & (mine_rank[None] == round_range[:, None, None, None])
    incoming_all = (
        jnp.sum(jnp.where(round_hit, request_head[None, None, :, None] + 1, 0), axis=2) - 1
    )
    query_groups = (
        query_rows.reshape(local_cubes, CUBE, head_count, head_size)
        .transpose(0, 2, 1, 3)
        .reshape(local_cubes * head_count, CUBE, head_size)
    )
    pair_blocks = jnp.concatenate(
        (
            key_rows.reshape(local_cubes, CUBE, head_count, head_size),
            value_rows.reshape(local_cubes, CUBE, head_count, head_size),
        ),
        axis=3,
    )
    pair_groups = pair_blocks.transpose(0, 2, 1, 3).reshape(
        local_cubes * head_count, CUBE, 2 * head_size
    )
    base_group = head_count * jnp.arange(local_cubes, dtype=jnp.int32)

    def held_pairs(incoming):
        source = (jnp.maximum(incoming, 0) + base_group[None, :]).reshape(-1)
        picked = jnp.take(pair_groups, source, axis=0)
        return jnp.where(
            (incoming >= 0).reshape(-1)[:, None, None], picked, jnp.zeros((), jnp.bfloat16)
        )

    def asked_queries(wanted):
        picked = jnp.take(query_groups, jnp.maximum(wanted, 0), axis=0)
        return jnp.where((wanted >= 0)[:, None, None], picked, jnp.zeros((), jnp.bfloat16))

    def one_round(state, tables):
        wanted, incoming = tables
        arrived = lax.all_to_all(
            held_pairs(incoming), "cubes", split_axis=0, concat_axis=0, tiled=True
        )
        results = block_partials(asked_queries(wanted), arrived)
        return (merge_slots(state, results, wanted), None)

    group_count = local_cubes * head_count
    start_state = (
        jnp.zeros((group_count, CUBE, head_size), jnp.float32),
        jnp.full((group_count, CUBE), NEG_START, jnp.float32),
        jnp.zeros((group_count, CUBE), jnp.float32),
    )
    final_state, unused = lax.scan(one_round, start_state, (wanted_all, incoming_all))
    numerator, running_max, totals = final_state
    fine_groups = numerator / totals[:, :, None]
    fine = (
        fine_groups.reshape(local_cubes, head_count, CUBE, head_size)
        .transpose(0, 2, 1, 3)
        .reshape(token_count, head_count, head_size)
    )
    gates = jax.nn.sigmoid(gate_logits.astype(jnp.float32))
    mixed = gates[:, :head_count, None] * coarse + gates[:, head_count:, None] * fine
    return mixed.reshape(token_count, feature_width).astype(jnp.bfloat16)

CORES = 2
HALVES = 2
SITES = 4
VMEM_GRANT = 62 * 1024 * 1024


def grid_of(device_count):
    chips = device_count // CORES
    x_extent = 1
    for extent in range(1, chips + 1):
        if chips % extent == 0 and extent**3 <= chips:
            x_extent = extent
    return (chips // x_extent, x_extent)


def attention_kernel(
    sizes,
    cube_ids_ref,
    selection_ref,
    query_rows,
    key_cubes,
    value_cubes,
    gate_columns,
    out_ref,
    *scratch,
):
    head_count, head_size, local_cubes, picks = sizes
    site_heads = head_count // SITES
    buffers = scratch[:site_heads]
    (stage, query_ref, gate_turned, gate_ref, done, out_block, position_ref) = scratch[
        site_heads : site_heads + 7
    ]
    (kv_send, kv_recv, query_send, query_recv, out_send, out_recv, kv_local, query_local) = scratch[
        site_heads + 7 :
    ]
    factor = 1.0 / math.sqrt(head_size)
    width = site_heads * head_size
    me = lax.axis_index("cubes")
    core = me % CORES
    x = (me // CORES) % 2
    low = (me // (2 * CORES)) % 2
    half = me // (4 * CORES)
    sibling = me + 1 - 2 * core

    def flip(bit, on):
        return bit + on * (1 - 2 * bit)

    def device(turn):
        return (
            (flip(half, turn // 4) * 2 + flip(low, (turn // 2) % 2)) * 2 + flip(x, turn % 2)
        ) * CORES + core

    def group(turn):
        return flip(x, turn % 2) * 2 + flip(low, (turn // 2) % 2)

    def head_columns(head, count):
        return pl.ds(pl.multiple_of(head * head_size, head_size), count * head_size)

    def cubes_of(source):
        return pl.ds(source * local_cubes, local_cubes)

    def remote(source, target, send, recv, partner):
        return pltpu.make_async_remote_copy(
            src_ref=source,
            dst_ref=target,
            send_sem=send,
            recv_sem=recv,
            device_id={"cubes": partner},
            device_id_type=pl.DeviceIdType.MESH,
        )

    def held(turn, inner):
        if turn % SITES == 0:
            return buffers[inner].at[cubes_of(me)]
        return stage.at[turn % SITES - 1, inner]

    def fills(turn, inner):
        columns = head_columns(group(turn) * site_heads + inner, 1)
        return [
            pltpu.make_async_copy(
                ref.at[:, :, columns], held(turn, inner).at[:, kind], kv_local.at[turn, inner, kind]
            )
            for kind, ref in enumerate((key_cubes, value_cubes))
        ]

    def own_queries():
        columns = head_columns(group(0) * site_heads, site_heads)
        return [
            pltpu.make_async_copy(query_rows.at[:, columns], query_ref.at[0], query_local.at[0]),
            pltpu.make_async_copy(gate_columns, gate_turned, query_local.at[1]),
        ]

    def query_copies(turn):
        columns = head_columns(group(turn) * site_heads, site_heads)
        return [
            remote(
                query_rows.at[:, columns],
                query_ref.at[turn],
                query_send.at[0, turn],
                query_recv.at[0, turn],
                device(turn),
            ),
            remote(
                gate_ref.at[0],
                gate_ref.at[turn],
                query_send.at[1, turn],
                query_recv.at[1, turn],
                device(turn),
            ),
        ]

    def kv_copy(turn, inner):
        return remote(
            held(turn, inner),
            buffers[inner].at[cubes_of(me)],
            kv_send.at[inner, turn],
            kv_recv.at[inner, turn],
            device(turn),
        )

    def kv_arrival(turn, inner):
        region = buffers[inner].at[cubes_of(device(turn))]
        return remote(
            region, region, kv_send.at[inner, turn], kv_recv.at[inner, turn], device(turn)
        )

    turns = SITES * HALVES

    def pass_on(turn, inner):
        region = buffers[inner].at[cubes_of(device(turn))]
        slot = turns + turn
        return remote(region, region, kv_send.at[inner, slot], kv_recv.at[inner, slot], sibling)

    def passed_arrival(turn, inner):
        region = buffers[inner].at[cubes_of(device(turn) + 1 - 2 * core)]
        slot = turns + turn
        return remote(region, region, kv_send.at[inner, slot], kv_recv.at[inner, slot], sibling)

    def out_copy(turn, inner):
        columns = head_columns(group(0) * site_heads + inner, 1)
        return remote(
            done.at[inner, turn],
            out_block.at[:, columns],
            out_send.at[inner, turn],
            out_recv.at[inner, turn],
            device(turn),
        )

    def out_arrival(turn, inner):
        columns = head_columns(group(turn) * site_heads + inner, 1)
        return remote(
            done.at[inner, turn],
            out_block.at[:, columns],
            out_send.at[inner, turn],
            out_recv.at[inner, turn],
            device(turn),
        )

    def compute(inner):
        buffer = buffers[inner]
        head = group(0) * site_heads + inner
        columns = slice(inner * head_size, (inner + 1) * head_size)

        def pooled(kind):
            cubes = buffer[:, kind].astype(jnp.float32)
            return (jnp.sum(cubes, axis=1) * (1.0 / CUBE)).astype(jnp.bfloat16)

        pooled_keys = pooled(0)
        pooled_values = pooled(1)

        def softmax(queries, keys, values):
            scores = (
                lax.dot_general(
                    queries, keys, (((1,), (1,)), ((), ())), preferred_element_type=jnp.float32
                )
                * factor
            )
            weights = jnp.exp(scores - jnp.max(scores, axis=1, keepdims=True))
            total = jnp.sum(weights, axis=1, keepdims=True)
            return (
                jnp.dot(weights.astype(jnp.bfloat16), values, preferred_element_type=jnp.float32)
                / total
            )

        def one_turn(turn):
            queries = query_ref[turn, :, columns]
            coarse = softmax(queries, pooled_keys, pooled_values)
            gates = gate_ref[turn].astype(jnp.float32)
            lane = lax.broadcasted_iota(jnp.int32, gates.shape, 1)
            coarse_gate = jax.nn.sigmoid(
                jnp.sum(jnp.where(lane == head, gates, 0.0), axis=1, keepdims=True)
            )
            fine_gate = jax.nn.sigmoid(
                jnp.sum(jnp.where(lane == head + head_count, gates, 0.0), axis=1, keepdims=True)
            )
            fine = []
            for cube in range(local_cubes):
                block = device(turn) * local_cubes + cube
                chosen = [position_ref[selection_ref[head, pick, block]] for pick in range(picks)]
                keys = jnp.concatenate([buffer[t, 0] for t in chosen], axis=0)
                values = jnp.concatenate([buffer[t, 1] for t in chosen], axis=0)
                fine.append(softmax(queries[cube * CUBE : (cube + 1) * CUBE], keys, values))
            fine = jnp.concatenate(fine, axis=0)
            return (coarse_gate * coarse + fine_gate * fine).astype(done.dtype)

        for pair in ((3, 2), (1, 0)):
            results = [one_turn(turn) for turn in pair]
            for turn, result in zip(pair, results):
                if turn == 0:
                    out_block[:, head_columns(head, 1)] = result
                else:
                    done[inner, turn] = result
            for turn in pair:
                if turn != 0:
                    out_copy(turn, inner).start()

    far_first = (7, 6, 5, 4, 3, 2, 1)

    def send(inner):
        for turn in range(SITES):
            for copy in fills(turn, inner):
                copy.wait()
        for turn in far_first:
            kv_copy(turn, inner).start()
        pass_on(0, inner).start()

    for copy in own_queries():
        copy.start()
    for inner in range(site_heads):
        for turn in range(SITES):
            for copy in fills(turn, inner):
                copy.start()
    barrier = pltpu.get_barrier_semaphore()
    for partner in [sibling] + [device(turn) for turn in range(1, turns)]:
        pl.semaphore_signal(
            barrier, inc=1, device_id={"cubes": partner}, device_id_type=pl.DeviceIdType.MESH
        )
    pl.semaphore_wait(barrier, turns)
    for copy in own_queries():
        copy.wait()
    gate_ref[0] = gate_turned[...].astype(jnp.float32).T.astype(gate_ref.dtype)
    for turn in range(1, SITES):
        for copy in query_copies(turn):
            copy.start()
    for inner in range(min(LOOKAHEAD, site_heads)):
        send(inner)

    def place(cube, carry):
        found = jnp.int32(0)
        for block in range(cube_ids_ref.shape[0]):
            found = jnp.where(cube_ids_ref[block] == cube, block, found)
        position_ref[cube] = found
        return carry

    lax.fori_loop(0, cube_ids_ref.shape[0], place, 0)
    for inner in range(site_heads):
        for turn in range(1, turns):
            kv_arrival(turn, inner).wait_recv()
            pass_on(turn, inner).start()
        if inner + LOOKAHEAD < site_heads:
            send(inner + LOOKAHEAD)
        if inner == 0:
            for turn in range(1, SITES):
                for copy in query_copies(turn):
                    copy.wait_recv()
        for turn in range(turns):
            passed_arrival(turn, inner).wait_recv()
        compute(inner)
    for inner in range(site_heads):
        for turn in range(1, SITES):
            out_arrival(turn, inner).wait_recv()
    out_ref[...] = out_block[...]
    for turn in range(1, SITES):
        for copy in query_copies(turn):
            copy.wait_send()
    for inner in range(site_heads):
        for turn in range(1, turns):
            kv_copy(turn, inner).wait_send()
        for turn in range(turns):
            pass_on(turn, inner).wait_send()
        for turn in range(1, SITES):
            out_copy(turn, inner).wait_send()


def gathered_body(query_rows, key_rows, value_rows, gate_logits, selection, cube_ids):
    token_count, feature_width = query_rows.shape
    head_count = gate_logits.shape[1] // 2
    head_size = feature_width // head_count
    local_cubes = token_count // CUBE
    total_cubes = cube_ids.shape[0]
    picks = selection.shape[2]
    site_heads = head_count // SITES
    turns = SITES * HALVES
    block = (local_cubes, 2, CUBE, head_size)
    return pl.pallas_call(
        functools.partial(attention_kernel, (head_count, head_size, local_cubes, picks)),
        out_shape=jax.ShapeDtypeStruct((token_count, feature_width), jnp.bfloat16),
        in_specs=[pl.BlockSpec(memory_space=pltpu.SMEM)] * 2
        + [pl.BlockSpec(memory_space=pltpu.HBM)] * 4,
        out_specs=pl.BlockSpec(memory_space=pltpu.VMEM),
        scratch_shapes=[
            pltpu.VMEM((total_cubes, 2, CUBE, head_size), jnp.bfloat16)
            for unused in range(site_heads)
        ]
        + [
            pltpu.VMEM((SITES - 1, site_heads) + block, jnp.bfloat16),
            pltpu.VMEM((SITES, token_count, site_heads * head_size), jnp.bfloat16),
            pltpu.VMEM(gate_logits.shape[::-1], jnp.bfloat16),
            pltpu.VMEM((SITES,) + gate_logits.shape, jnp.bfloat16),
            pltpu.VMEM((site_heads, SITES, token_count, head_size), jnp.bfloat16),
            pltpu.VMEM((token_count, feature_width), jnp.bfloat16),
            pltpu.SMEM((total_cubes,), jnp.int32),
            pltpu.SemaphoreType.DMA((site_heads, 2 * turns)),
            pltpu.SemaphoreType.DMA((site_heads, 2 * turns)),
            pltpu.SemaphoreType.DMA((2, SITES)),
            pltpu.SemaphoreType.DMA((2, SITES)),
            pltpu.SemaphoreType.DMA((site_heads, SITES)),
            pltpu.SemaphoreType.DMA((site_heads, SITES)),
            pltpu.SemaphoreType.DMA((SITES, site_heads, 2)),
            pltpu.SemaphoreType.DMA((2,)),
        ],
        compiler_params=pltpu.CompilerParams(
            collective_id=0, has_side_effects=True, vmem_limit_bytes=VMEM_GRANT
        ),
    )(
        cube_ids,
        selection.transpose(1, 2, 0),
        query_rows,
        key_rows.reshape(local_cubes, CUBE, feature_width),
        value_rows.reshape(local_cubes, CUBE, feature_width),
        gate_logits.T,
    )


def body(query_rows, key_rows, value_rows, gate_logits, selection, cube_ids):
    device_count = lax.axis_size("cubes")
    head_count = gate_logits.shape[1] // 2
    fits = (
        device_count == CORES * SITES * HALVES
        and grid_of(device_count) == (2 * HALVES, SITES // 2)
        and head_count % SITES == 0
    )
    return (gathered_body if fits else streamed_body)(
        query_rows, key_rows, value_rows, gate_logits, selection, cube_ids
    )


def solution(mesh):
    placed = (
        P(("groups", "cubes"), None),
        P(("groups", "cubes"), None),
        P(("groups", "cubes"), None),
        P(("groups", "cubes"), None),
        P("groups", None, None),
        P("groups"),
    )
    return jax.shard_map(
        body, mesh=mesh, in_specs=placed, out_specs=P(("groups", "cubes"), None), check_vma=False
    )
```
